256 devices in a mesh: ctx: 128 (over x_hi, z, y, core), ch: 2 (over x_lo).
Axes of the slice: x: 4 (x_hi: 2, x_lo: 2; x = x_hi * 2 + x_lo), y: 4, z: 8, core: 2. Of those that a mesh axis runs over, the one named last changes fastest.
Arguments:
- query_proj: bfloat16 [128, 32768], P('ch', 'ctx'), may hold values from -6 to 6
- key_proj: bfloat16 [128, 32768], P('ch', 'ctx'), may hold values from -6 to 6
- value_proj: bfloat16 [128, 32768], P('ch', 'ctx'), may hold values from -6 to 6
- filter_taps: float32 [32768], P('ctx'), may hold values from -0.03125 to 0.03125
- out_grad: bfloat16 [128, 32768], P('ch', 'ctx'), may hold values from -6 to 6
Outputs:
- query_grad: bfloat16 [128, 32768], P('ch', 'ctx')
- key_grad: bfloat16 [128, 32768], P('ch', 'ctx')
- value_grad: bfloat16 [128, 32768], P('ch', 'ctx')
- filter_grad: float32 [32768], P('ctx')
The draws below stay inside these ranges and needn't reach their ends.
All inputs are finite; a program needn't handle non-finite values.
Results may differ from the reference program's by a relative error of at most 0.0033.
Values sent between devices are 32-bit elements; how exact they have to be, the bound alone decides.
No kernel may reach another device: no remote copies, remote signals or barrier semaphores. Data moves between devices by JAX's collectives and lax.ppermute only.
A program may use at most 64 MiB of HBM per device.

```python
import math
import jax
import jax.numpy as jnp
from jax import lax

C = 128
TOKENS = 32768
PADDED = 65536


def level_of(rng, extent, cuts, least, largest):
    def one(position, parts):
        steps = jax.random.uniform(jax.random.fold_in(jax.random.fold_in(rng, 6), position), (parts,), jnp.float32, least / len(cuts), largest / len(cuts))
        return jnp.repeat(jnp.exp(steps), extent[position] // parts).reshape((-1,) + (1,) * (len(extent) - position - 1))

    factor_of = one(*cuts[0])
    for cut in cuts[1:]:
        factor_of = factor_of * one(*cut)
    return factor_of


def scatter_about(rng, dims, scale, reach, shards=(), kind=jnp.bfloat16):
    factor_of = level_of(rng, dims, shards, -0.22, 0.18) if shards else 1.0
    result = jax.random.normal(rng, dims, jnp.float32) * scale * factor_of
    return jnp.minimum(jnp.maximum(result, -reach), reach).astype(kind)


def setup_inputs(seed: int = 0) -> dict:
    key_list = jax.random.split(jax.random.key(seed), 6)
    query_proj = scatter_about(key_list[0], (C, TOKENS), 1.0, 6.0, ((0, 2), (1, 128)))
    key_proj = scatter_about(key_list[1], (C, TOKENS), 1.0, 6.0, ((0, 2), (1, 128)))
    value_proj = scatter_about(key_list[2], (C, TOKENS), 1.0, 6.0, ((0, 2), (1, 128)))
    filter_taps = scatter_about(key_list[3], (TOKENS,), TOKENS ** -0.5, 0.03125, ((0, 128),), jnp.float32)
    out_grad = scatter_about(key_list[4], (C, TOKENS), 1.0, 6.0, ((0, 2), (1, 128)))
    return dict(query_proj=query_proj, key_proj=key_proj, value_proj=value_proj, filter_taps=filter_taps, out_grad=out_grad)


def reference(query_proj, key_proj, value_proj, filter_taps, out_grad):
    width = math.gcd(C, 16)
    filter_spectrum = jnp.fft.rfft(filter_taps.astype(jnp.float32), n=PADDED)

    def one_block(pieces):
        query_rows, key_rows, value_rows, grad_rows = pieces
        gated = key_rows.astype(jnp.float32) * value_rows.astype(jnp.float32)
        gate_grad = grad_rows.astype(jnp.float32) * query_rows.astype(jnp.float32)
        gated_spectrum = jnp.fft.rfft(gated, n=PADDED, axis=-1)
        grad_spectrum = jnp.fft.rfft(gate_grad, n=PADDED, axis=-1)
        conv_out = jnp.fft.irfft(gated_spectrum * filter_spectrum, n=PADDED, axis=-1)[:, :TOKENS]
        back_out = jnp.fft.irfft(grad_spectrum * jnp.conj(filter_spectrum), n=PADDED, axis=-1)[:, :TOKENS]
        cross = lax.optimization_barrier(jnp.sum(grad_spectrum * jnp.conj(gated_spectrum), axis=0))
        query_grad = (grad_rows.astype(jnp.float32) * conv_out).astype(jnp.bfloat16)
        key_grad = (back_out * value_rows.astype(jnp.float32)).astype(jnp.bfloat16)
        value_grad = (back_out * key_rows.astype(jnp.float32)).astype(jnp.bfloat16)
        return (query_grad, key_grad, value_grad, cross)
    blocks = (query_proj.reshape(C // width, width, TOKENS), key_proj.reshape(C // width, width, TOKENS), value_proj.reshape(C // width, width, TOKENS), out_grad.reshape(C // width, width, TOKENS))
    query_grad, key_grad, value_grad, crosses = lax.map(one_block, blocks)
    cross_spectrum = lax.optimization_barrier(jnp.sum(crosses, axis=0))
    filter_grad = jnp.fft.irfft(cross_spectrum, n=PADDED)[:TOKENS] * (1.0 / math.sqrt(C * TOKENS))
    return (query_grad.reshape(C, TOKENS), key_grad.reshape(C, TOKENS), value_grad.reshape(C, TOKENS), filter_grad.astype(jnp.float32))
```

```python
import math

import jax
import jax.numpy as jnp
import numpy as np
from jax import lax
from jax.experimental import pallas as pl
from jax.experimental.pallas import tpu as pltpu
from jax.sharding import PartitionSpec as P

SHIFT = 0.25


def halves(values):
    high = values.astype(jnp.bfloat16)
    low = (values - np.asarray(high).astype(np.float64)).astype(jnp.bfloat16)
    return np.asarray(high), np.asarray(low)


def tables(blocks, width):
    length = blocks * width
    rows = np.arange(blocks) + SHIFT
    block_angle = 2.0 * math.pi * np.outer(rows, np.arange(blocks)) / blocks
    forward = np.concatenate([np.cos(block_angle), -np.sin(block_angle)], axis=0)
    backward = np.concatenate([np.cos(block_angle), -np.sin(block_angle)], axis=0).T / length
    own = [np.arange(parity, blocks, 2) for parity in (0, 1)]
    ahead = np.stack([np.concatenate([forward[:, own[e]], forward[:, own[1 - e]]], 1) for e in (0, 1)])
    back = np.stack([backward[own[e], :] for e in (0, 1)])
    ahead_high, ahead_low = halves(ahead)
    back_high, back_low = halves(back)
    ahead_table = np.concatenate([ahead_high, ahead_high, ahead_low], axis=2)
    back_table = np.concatenate([back_high, back_high, back_low], axis=2)
    twist_angle = 2.0 * math.pi * np.outer(rows, np.arange(width)) / length
    twist = np.stack([np.cos(twist_angle), np.sin(twist_angle)]).astype(np.float32)
    inner_angle = 2.0 * math.pi * (np.outer(np.arange(width), np.arange(width)) % width) / width
    inner_high, inner_low = halves(np.concatenate([np.cos(inner_angle), np.sin(inner_angle)], axis=1))
    return ahead_table, back_table, twist, np.stack([inner_high, inner_low])


def split(values):
    high = values.astype(jnp.bfloat16)
    return high, (values - high.astype(jnp.float32)).astype(jnp.bfloat16)


def dot(left, right):
    return jnp.dot(left, right, preferred_element_type=jnp.float32)


def inner_dot(values, inner_ref):
    high, low = split(values)
    return dot(high, inner_ref[0]) + dot(low, inner_ref[0]) + dot(high, inner_ref[1])


def pack_body(query_ref, key_ref, value_ref, grad_ref, taps_ref, out_ref):
    width = query_ref.shape[1]
    out_ref[:, 0, :width] = key_ref[...].astype(jnp.float32) * value_ref[...].astype(jnp.float32)
    out_ref[:, 0, width : 2 * width] = grad_ref[...].astype(jnp.float32) * query_ref[...].astype(jnp.float32)
    out_ref[:, 0, 2 * width :] = jnp.broadcast_to(taps_ref[...], query_ref.shape)


def middle_body(scale, parity_ref, own_ref, other_ref, ahead_ref, back_ref, twist_ref, inner_ref, out_ref):
    parity = parity_ref[0]
    width = twist_ref.shape[2]
    rows = twist_ref.shape[1]
    signal = jnp.concatenate([own_ref[:, 0, :], other_ref[:, 0, :]], axis=0)
    high, low = split(signal)
    front = dot(ahead_ref[parity], jnp.concatenate([high, low, high], axis=0))
    cosine, sine = twist_ref[0], twist_ref[1]
    turned = []
    for index in range(3):
        real = front[:rows, index * width : (index + 1) * width]
        imag = front[rows:, index * width : (index + 1) * width]
        turned += [real * cosine + imag * sine, imag * cosine - real * sine]
    product = inner_dot(jnp.concatenate(turned, axis=0), inner_ref)
    spectra = []
    for index in range(3):
        real = product[2 * index * rows : (2 * index + 1) * rows]
        imag = product[(2 * index + 1) * rows : (2 * index + 2) * rows]
        spectra.append((real[:, :width] + imag[:, width:], imag[:, :width] - real[:, width:]))
    (gated_real, gated_imag), (grad_real, grad_imag), (taps_real, taps_imag) = spectra
    mixed = [
        gated_real * taps_real - gated_imag * taps_imag,
        gated_real * taps_imag + gated_imag * taps_real,
        grad_real * taps_real + grad_imag * taps_imag,
        grad_imag * taps_real - grad_real * taps_imag,
        (grad_real * gated_real + grad_imag * gated_imag) * scale,
        (grad_imag * gated_real - grad_real * gated_imag) * scale,
    ]
    product = inner_dot(jnp.concatenate(mixed, axis=0), inner_ref)
    waves = []
    for index in range(3):
        real = product[2 * index * rows : (2 * index + 1) * rows]
        imag = product[(2 * index + 1) * rows : (2 * index + 2) * rows]
        wave_real = real[:, :width] - imag[:, width:]
        wave_imag = imag[:, :width] + real[:, width:]
        waves.append(
            jnp.concatenate([wave_real * cosine - wave_imag * sine, wave_real * sine + wave_imag * cosine], axis=0)
        )
    high, low = split(jnp.concatenate(waves, axis=1))
    out_ref[:, 0, :] = dot(back_ref[parity], jnp.concatenate([high, low, high], axis=0))


def finish_body(moved_ref, key_ref, value_ref, grad_ref, query_out, key_out, value_out, filter_out):
    width = key_ref.shape[1]
    conv = moved_ref[:, 0, :width]
    back = moved_ref[:, 0, width : 2 * width]
    query_out[...] = (grad_ref[...].astype(jnp.float32) * conv).astype(jnp.bfloat16)
    key_out[...] = (back * value_ref[...].astype(jnp.float32)).astype(jnp.bfloat16)
    value_out[...] = (back * key_ref[...].astype(jnp.float32)).astype(jnp.bfloat16)
    filter_out[...] = jnp.sum(moved_ref[:, 0, 2 * width :], axis=0, keepdims=True)


def shards(query_proj, key_proj, value_proj, filter_taps, out_grad):
    devices = lax.axis_size("ctx")
    channels, width = query_proj.shape
    chips = devices // 2
    parity = (lax.axis_index("ctx") % 2).astype(jnp.int32).reshape(1)
    same_core = [[2 * chip + core for chip in range(chips)] for core in (0, 1)]
    other_core = [(device, device ^ 1) for device in range(devices)]
    total = channels * lax.axis_size("ch") * devices * width
    message = jax.ShapeDtypeStruct((chips, 1, 3 * width), jnp.float32)

    def exchange(array):
        return lax.all_to_all(array, "ctx", 0, 0, axis_index_groups=same_core, tiled=True)

    packed = pl.pallas_call(pack_body, out_shape=message)(
        query_proj, key_proj, value_proj, out_grad, filter_taps.reshape(1, width)
    )
    own = exchange(packed)
    other = lax.ppermute(own, "ctx", other_core)
    in_smem = pl.BlockSpec(memory_space=pltpu.SMEM)
    in_vmem = pl.BlockSpec(memory_space=pltpu.VMEM)
    constants = [jnp.asarray(table) for table in tables(devices, width)]

    def middle(*refs):
        middle_body(1.0 / math.sqrt(total), *refs)

    restored = pl.pallas_call(
        middle,
        out_shape=message,
        in_specs=[in_smem] + [in_vmem] * 6,
        out_specs=in_vmem,
        compiler_params=pltpu.CompilerParams(vmem_limit_bytes=40 * 1024 * 1024),
    )(parity, own, other, *constants)
    moved = exchange(restored)
    narrow = jax.ShapeDtypeStruct((channels, width), jnp.bfloat16)
    query_grad, key_grad, value_grad, partial = pl.pallas_call(
        finish_body,
        out_shape=(narrow, narrow, narrow, jax.ShapeDtypeStruct((1, width), jnp.float32)),
    )(moved, key_proj, value_proj, out_grad)
    partial = partial.reshape(width)
    filter_grad = partial + lax.ppermute(partial, "ch", [(0, 1), (1, 0)])
    return (query_grad, key_grad, value_grad, filter_grad)


def solution(mesh):
    placed = (P("ch", "ctx"), P("ch", "ctx"), P("ch", "ctx"), P("ctx"), P("ch", "ctx"))
    return jax.shard_map(
        shards,
        mesh=mesh,
        in_specs=placed,
        out_specs=(P("ch", "ctx"), P("ch", "ctx"), P("ch", "ctx"), P("ctx")),
        check_vma=False,
    )
```

```python
import math

import jax
import jax.numpy as jnp
import numpy as np
from jax import lax
from jax.experimental import pallas as pl
from jax.experimental.pallas import tpu as pltpu
from jax.sharding import PartitionSpec as P

SHIFT = 0.25
MIB = 1024 * 1024
AHEAD, BACK, TWIST = 4, 8, 9


def halves(values):
    high = values.astype(jnp.bfloat16)
    low = (values - np.asarray(high).astype(np.float64)).astype(jnp.bfloat16)
    return np.asarray(high), np.asarray(low)


def table_bank(blocks, width):
    length = blocks * width
    half = width // 2
    rows = np.arange(blocks) + SHIFT
    planes = []
    for odd in (0, 1):
        angle = 2.0 * math.pi * (np.outer(np.arange(half), 2 * np.arange(half) + odd) % width) / width
        cosine, sine = np.cos(angle), np.sin(angle)
        planes += halves(np.block([[cosine, -sine], [sine, cosine]]))
    block_angle = 2.0 * math.pi * np.outer(rows, np.arange(blocks)) / blocks
    block_table = np.concatenate([np.cos(block_angle), -np.sin(block_angle)], axis=0)
    own = [np.arange(parity, blocks, 2) for parity in (0, 1)]
    for e in (0, 1):
        high, low = halves(np.concatenate([block_table[:, own[e]], block_table[:, own[1 - e]]], axis=1))
        planes += [np.concatenate([high, high], axis=1), np.concatenate([low, np.zeros_like(low)], axis=1)]
    pieces = [np.concatenate(halves(block_table.T[own[e]] / length), axis=0) for e in (0, 1)]
    planes.append(np.concatenate(pieces, axis=0))
    twist_angle = 2.0 * math.pi * np.outer(rows, np.arange(width)) / length
    planes += [np.concatenate(halves(np.cos(twist_angle)), axis=0), np.concatenate(halves(np.sin(twist_angle)), axis=0)]
    return np.stack(planes)


def split(values):
    high = values.astype(jnp.bfloat16)
    return high, (values - high.astype(jnp.float32)).astype(jnp.bfloat16)


def product(left, right, transposed=False):
    contracted = (((1,), (1 if transposed else 0,)), ((), ()))
    return lax.dot_general(left, right, contracted, preferred_element_type=jnp.float32)


def inner_product(values, bank_ref, odd, transposed):
    count = values.shape[0]
    high, low = split(values)
    wide = product(jnp.concatenate([high, low], axis=0), bank_ref[2 * odd], transposed)
    return wide[:count] + wide[count:] + product(high, bank_ref[2 * odd + 1], transposed)


def pack_body(query_ref, key_ref, value_ref, grad_ref, taps_ref, out_ref):
    width = query_ref.shape[1]
    out_ref[:, 0, :width] = key_ref[...].astype(jnp.float32) * value_ref[...].astype(jnp.float32)
    out_ref[:, 0, width : 2 * width] = grad_ref[...].astype(jnp.float32) * query_ref[...].astype(jnp.float32)
    out_ref[:, 0, 2 * width :] = jnp.broadcast_to(taps_ref[...], query_ref.shape)


def middle_body(scale, parity_ref, own_ref, other_ref, bank_ref, out_ref):
    parity = parity_ref[0]
    width = bank_ref.shape[2]
    half = width // 2
    rows = 2 * own_ref.shape[0]
    high, low = split(jnp.concatenate([own_ref[:, 0, :], other_ref[:, 0, :]], axis=0))
    ahead = bank_ref[pl.ds(AHEAD + 2 * parity, 2)].reshape(2 * width, width)
    front = product(ahead, jnp.concatenate([high, low], axis=0))
    front = front[: 2 * rows] + front[2 * rows :]
    twist = [bank_ref[TWIST + i].astype(jnp.float32) for i in (0, 1)]
    cosine, sine = [table[:rows] + table[rows:] for table in twist]
    even, odd = [], []
    for index in range(3):
        real = front[:rows, index * width : (index + 1) * width]
        imag = front[rows:, index * width : (index + 1) * width]
        real, imag = real * cosine + imag * sine, imag * cosine - real * sine
        even.append(jnp.concatenate([real[:, :half] + real[:, half:], imag[:, :half] + imag[:, half:]], axis=1))
        odd.append(jnp.concatenate([real[:, :half] - real[:, half:], imag[:, :half] - imag[:, half:]], axis=1))
    waves = []
    for bins, stacked in enumerate((even, odd)):
        spectra = inner_product(jnp.concatenate(stacked, axis=0), bank_ref, bins, False)
        gated_real, gated_imag = spectra[:rows, :half], spectra[:rows, half:]
        grad_real, grad_imag = spectra[rows : 2 * rows, :half], spectra[rows : 2 * rows, half:]
        taps_real, taps_imag = spectra[2 * rows :, :half], spectra[2 * rows :, half:]
        conv_real = gated_real * taps_real - gated_imag * taps_imag
        conv_imag = gated_real * taps_imag + gated_imag * taps_real
        back_real = grad_real * taps_real + grad_imag * taps_imag
        back_imag = grad_imag * taps_real - grad_real * taps_imag
        cross_real = (grad_real * gated_real + grad_imag * gated_imag) * scale
        cross_imag = (grad_imag * gated_real - grad_real * gated_imag) * scale
        mixed = jnp.concatenate(
            [
                jnp.concatenate([conv_real, conv_imag], axis=1),
                jnp.concatenate([back_real, back_imag], axis=1),
                jnp.concatenate([cross_real, cross_imag], axis=1),
            ],
            axis=0,
        )
        waves.append(inner_product(mixed, bank_ref, bins, True))
    turned = []
    for index in range(3):
        first = waves[0][index * rows : (index + 1) * rows]
        second = waves[1][index * rows : (index + 1) * rows]
        total, difference = first + second, first - second
        real = jnp.concatenate([total[:, :half], difference[:, :half]], axis=1)
        imag = jnp.concatenate([total[:, half:], difference[:, half:]], axis=1)
        turned.append(jnp.concatenate([real * cosine - imag * sine, real * sine + imag * cosine], axis=0))
    high, low = split(jnp.concatenate(turned, axis=1))
    table = bank_ref[BACK, pl.ds(pl.multiple_of(rows * parity, rows), rows)]
    wide = product(table, high)
    out_ref[:, 0, :] = wide[: rows // 2] + wide[rows // 2 :] + product(table[: rows // 2], low)


def sum_body(moved_ref, out_ref):
    width = out_ref.shape[1]
    out_ref[...] = jnp.sum(moved_ref[:, 0, 2 * width :], axis=0, keepdims=True)


def finish_body(moved_ref, key_ref, value_ref, grad_ref, query_out, key_out, value_out):
    width = key_ref.shape[1]
    conv = moved_ref[:, 0, :width]
    back = moved_ref[:, 0, width : 2 * width]
    query_out[...] = (grad_ref[...].astype(jnp.float32) * conv).astype(jnp.bfloat16)
    key_out[...] = (back * value_ref[...].astype(jnp.float32)).astype(jnp.bfloat16)
    value_out[...] = (back * key_ref[...].astype(jnp.float32)).astype(jnp.bfloat16)


def kernel_call(body, out_shape, limit, operands, in_specs=None):
    placed = {} if in_specs is None else {"in_specs": in_specs}
    return pl.pallas_call(
        body,
        out_shape=out_shape,
        compiler_params=pltpu.CompilerParams(vmem_limit_bytes=limit * MIB),
        **placed,
    )(*operands)


def shards(query_proj, key_proj, value_proj, filter_taps, out_grad):
    devices = lax.axis_size("ctx")
    channels, width = query_proj.shape
    chips = devices // 2
    parity = (lax.axis_index("ctx") % 2).astype(jnp.int32).reshape(1)
    same_core = [[2 * chip + core for chip in range(chips)] for core in (0, 1)]
    other_core = [(device, device ^ 1) for device in range(devices)]
    scale = 1.0 / math.sqrt(channels * lax.axis_size("ch") * devices * width)
    message = jax.ShapeDtypeStruct((chips, 1, 3 * width), jnp.float32)
    narrow = jax.ShapeDtypeStruct((channels, width), jnp.bfloat16)
    bank = jnp.asarray(table_bank(devices, width))

    def exchange(array):
        return lax.all_to_all(array, "ctx", 0, 0, axis_index_groups=same_core, tiled=True)

    def middle(*refs):
        middle_body(scale, *refs)

    taps = filter_taps.reshape(1, width)
    packed = kernel_call(pack_body, message, 4, (query_proj, key_proj, value_proj, out_grad, taps))
    own = exchange(packed)
    other = lax.ppermute(own, "ctx", other_core)
    in_smem = pl.BlockSpec(memory_space=pltpu.SMEM)
    in_vmem = pl.BlockSpec(memory_space=pltpu.VMEM)
    restored = kernel_call(middle, message, 24, (parity, own, other, bank), [in_smem, in_vmem, in_vmem, in_vmem])
    moved = exchange(restored)
    partial = kernel_call(sum_body, jax.ShapeDtypeStruct((1, width), jnp.float32), 4, (moved,)).reshape(width)
    swapped = lax.ppermute(partial, "ch", [(0, 1), (1, 0)])
    query_grad, key_grad, value_grad = kernel_call(
        finish_body, (narrow, narrow, narrow), 4, (moved, key_proj, value_proj, out_grad)
    )
    return (query_grad, key_grad, value_grad, partial + swapped)


def solution(mesh):
    placed = (P("ch", "ctx"), P("ch", "ctx"), P("ch", "ctx"), P("ctx"), P("ch", "ctx"))
    return jax.shard_map(
        shards,
        mesh=mesh,
        in_specs=placed,
        out_specs=(P("ch", "ctx"), P("ch", "ctx"), P("ch", "ctx"), P("ctx")),
        check_vma=False,
    )
```

```python
import math

import jax
import jax.numpy as jnp
import numpy as np
from jax import lax
from jax.experimental import pallas as pl
from jax.experimental.pallas import tpu as pltpu
from jax.sharding import PartitionSpec as P

SHIFT = 0.25
MIB = 1024 * 1024
AHEAD, BACK, TWIST = 4, 8, 9


def halves(values):
    high = values.astype(jnp.bfloat16)
    low = (values - np.asarray(high).astype(np.float64)).astype(jnp.bfloat16)
    return np.asarray(high), np.asarray(low)


def table_bank(blocks, width):
    length = blocks * width
    half = width // 2
    rows = np.arange(blocks) + SHIFT
    planes = []
    for odd in (0, 1):
        angle = 2.0 * math.pi * (np.outer(np.arange(half), 2 * np.arange(half) + odd) % width) / width
        cosine, sine = np.cos(angle), np.sin(angle)
        planes += halves(np.block([[cosine, -sine], [sine, cosine]]))
    block_angle = 2.0 * math.pi * np.outer(rows, np.arange(blocks)) / blocks
    block_table = np.concatenate([np.cos(block_angle), -np.sin(block_angle)], axis=0)
    own = [np.arange(parity, blocks, 2) for parity in (0, 1)]
    for e in (0, 1):
        high, low = halves(np.concatenate([block_table[:, own[e]], block_table[:, own[1 - e]]], axis=1))
        planes += [np.concatenate([high, high], axis=1), np.concatenate([low, np.zeros_like(low)], axis=1)]
    pieces = [np.concatenate(halves(block_table.T[own[e]] / length), axis=0) for e in (0, 1)]
    planes.append(np.concatenate(pieces, axis=0))
    twist_angle = 2.0 * math.pi * np.outer(rows, np.arange(width)) / length
    planes += [np.concatenate(halves(np.cos(twist_angle)), axis=0), np.concatenate(halves(np.sin(twist_angle)), axis=0)]
    return np.stack(planes)


def split(values):
    high = values.astype(jnp.bfloat16)
    return high, (values - high.astype(jnp.float32)).astype(jnp.bfloat16)


def product(left, right, transposed=False):
    contracted = (((1,), (1 if transposed else 0,)), ((), ()))
    return lax.dot_general(left, right, contracted, preferred_element_type=jnp.float32)


def inner_product(values, bank_ref, odd, transposed):
    count = values.shape[0]
    high, low = split(values)
    wide = product(jnp.concatenate([high, low], axis=0), bank_ref[2 * odd], transposed)
    return wide[:count] + wide[count:] + product(high, bank_ref[2 * odd + 1], transposed)


def fetch(pairs, arrived):
    copies = [pltpu.make_async_copy(source, here, arrived.at[i]) for i, (source, here) in enumerate(pairs)]
    for copy in copies:
        copy.start()
    return copies


def pack_body(key_far, value_far, grad_far, query_far, taps_far, out_ref, key, value, grad, query, taps, arrived):
    width = key.shape[1]
    copies = fetch(
        ((key_far, key), (value_far, value), (grad_far, grad), (query_far, query), (taps_far, taps)), arrived
    )
    copies[0].wait()
    copies[1].wait()
    out_ref[:, 0, :width] = key[...].astype(jnp.float32) * value[...].astype(jnp.float32)
    copies[2].wait()
    copies[3].wait()
    out_ref[:, 0, width : 2 * width] = grad[...].astype(jnp.float32) * query[...].astype(jnp.float32)
    copies[4].wait()
    out_ref[:, 0, 2 * width :] = jnp.broadcast_to(taps[...], key.shape)


def lead_body(own_ref, bank_far, bank_ref, arrived):
    for copy in fetch([(bank_far, bank_ref)], arrived):
        copy.wait()


def middle_body(scale, parity_ref, own_ref, other_ref, bank_ref, out_ref):
    parity = parity_ref[0]
    width = bank_ref.shape[2]
    half = width // 2
    rows = 2 * own_ref.shape[0]
    ahead = bank_ref[pl.ds(AHEAD + 2 * parity, 2)].reshape(2 * width, width)
    signal = jnp.concatenate([own_ref[:, 0, :], other_ref[:, 0, :]], axis=0)
    front = product(ahead, jnp.concatenate(split(signal), axis=0))
    front = front[: 2 * rows] + front[2 * rows :]
    twist = [bank_ref[TWIST + i].astype(jnp.float32) for i in (0, 1)]
    cosine, sine = [table[:rows] + table[rows:] for table in twist]
    even, odd = [], []
    for index in range(3):
        real = front[:rows, index * width : (index + 1) * width]
        imag = front[rows:, index * width : (index + 1) * width]
        real, imag = real * cosine + imag * sine, imag * cosine - real * sine
        even.append(jnp.concatenate([real[:, :half] + real[:, half:], imag[:, :half] + imag[:, half:]], axis=1))
        odd.append(jnp.concatenate([real[:, :half] - real[:, half:], imag[:, :half] - imag[:, half:]], axis=1))
    waves = []
    for bins, stacked in enumerate((even, odd)):
        spectra = inner_product(jnp.concatenate(stacked, axis=0), bank_ref, bins, False)
        gated_real, gated_imag = spectra[:rows, :half], spectra[:rows, half:]
        grad_real, grad_imag = spectra[rows : 2 * rows, :half], spectra[rows : 2 * rows, half:]
        taps_real, taps_imag = spectra[2 * rows :, :half], spectra[2 * rows :, half:]
        conv_real = gated_real * taps_real - gated_imag * taps_imag
        conv_imag = gated_real * taps_imag + gated_imag * taps_real
        back_real = grad_real * taps_real + grad_imag * taps_imag
        back_imag = grad_imag * taps_real - grad_real * taps_imag
        cross_real = (grad_real * gated_real + grad_imag * gated_imag) * scale
        cross_imag = (grad_imag * gated_real - grad_real * gated_imag) * scale
        mixed = jnp.concatenate(
            [
                jnp.concatenate([conv_real, conv_imag], axis=1),
                jnp.concatenate([back_real, back_imag], axis=1),
                jnp.concatenate([cross_real, cross_imag], axis=1),
            ],
            axis=0,
        )
        waves.append(inner_product(mixed, bank_ref, bins, True))
    turned = []
    for index in range(3):
        first = waves[0][index * rows : (index + 1) * rows]
        second = waves[1][index * rows : (index + 1) * rows]
        total, difference = first + second, first - second
        real = jnp.concatenate([total[:, :half], difference[:, :half]], axis=1)
        imag = jnp.concatenate([total[:, half:], difference[:, half:]], axis=1)
        turned.append(jnp.concatenate([real * cosine - imag * sine, real * sine + imag * cosine], axis=0))
    high, low = split(jnp.concatenate(turned, axis=1))
    table = bank_ref[BACK, pl.ds(pl.multiple_of(rows * parity, rows), rows)]
    wide = product(table, high)
    out_ref[:, 0, :] = wide[: rows // 2] + wide[rows // 2 :] + product(table[: rows // 2], low)


def sum_body(moved_ref, out_ref):
    width = out_ref.shape[1]
    out_ref[...] = jnp.sum(moved_ref[:, 0, 2 * width :], axis=0, keepdims=True)


def finish_body(moved_ref, grad_far, value_far, key_far, query_out, key_out, value_out, grad, value, key, arrived):
    width = key.shape[1]
    copies = fetch(((grad_far, grad), (value_far, value), (key_far, key)), arrived)
    back = moved_ref[:, 0, width : 2 * width]
    copies[0].wait()
    query_out[...] = (grad[...].astype(jnp.float32) * moved_ref[:, 0, :width]).astype(jnp.bfloat16)
    copies[1].wait()
    key_out[...] = (back * value[...].astype(jnp.float32)).astype(jnp.bfloat16)
    copies[2].wait()
    value_out[...] = (back * key[...].astype(jnp.float32)).astype(jnp.bfloat16)


def add_body(left_ref, right_ref, out_ref):
    out_ref[...] = left_ref[...] + right_ref[...]


def kernel_call(body, out_shape, limit, operands, in_specs, scratch=()):
    return pl.pallas_call(
        body,
        out_shape=out_shape,
        in_specs=in_specs,
        scratch_shapes=scratch,
        compiler_params=pltpu.CompilerParams(vmem_limit_bytes=limit * MIB),
    )(*operands)


def shards(query_proj, key_proj, value_proj, filter_taps, out_grad):
    devices = lax.axis_size("ctx")
    channels, width = query_proj.shape
    chips = devices // 2
    parity = (lax.axis_index("ctx") % 2).astype(jnp.int32).reshape(1)
    same_core = [[2 * chip + core for chip in range(chips)] for core in (0, 1)]
    other_core = [(device, device ^ 1) for device in range(devices)]
    scale = 1.0 / math.sqrt(channels * lax.axis_size("ch") * devices * width)
    message = jax.ShapeDtypeStruct((chips, 1, 3 * width), jnp.float32)
    narrow = jax.ShapeDtypeStruct((channels, width), jnp.bfloat16)
    bank = jnp.asarray(table_bank(devices, width))

    def exchange(array):
        return lax.all_to_all(array, "ctx", 0, 0, axis_index_groups=same_core, tiled=True)

    def middle(*refs):
        middle_body(scale, *refs)

    far = pl.BlockSpec(memory_space=pltpu.HBM)
    key_far, value_far, grad_far, query_far, taps_far = [
        pltpu.with_memory_space_constraint(array, pltpu.HBM)
        for array in (key_proj, value_proj, out_grad, query_proj, filter_taps.reshape(1, width))
    ]
    near = pl.BlockSpec(memory_space=pltpu.VMEM)
    scalar = pl.BlockSpec(memory_space=pltpu.SMEM)
    local = pltpu.VMEM((channels, width), jnp.bfloat16)
    packed = kernel_call(
        pack_body,
        message,
        4,
        (key_far, value_far, grad_far, query_far, taps_far),
        [far] * 5,
        [local] * 4 + [pltpu.VMEM((1, width), jnp.float32), pltpu.SemaphoreType.DMA((5,))],
    )
    own = exchange(packed)
    other = lax.ppermute(own, "ctx", other_core)
    near_bank = kernel_call(
        lead_body,
        jax.ShapeDtypeStruct(bank.shape, bank.dtype),
        8,
        (own, pltpu.with_memory_space_constraint(bank, pltpu.HBM)),
        [near, far],
        [pltpu.SemaphoreType.DMA((1,))],
    )
    restored = kernel_call(middle, message, 24, (parity, own, other, near_bank), [scalar, near, near, near])
    moved = exchange(restored)
    line = jax.ShapeDtypeStruct((1, width), jnp.float32)
    partial = kernel_call(sum_body, line, 4, (moved,), [near])
    swapped = lax.ppermute(partial, "ch", [(0, 1), (1, 0)])
    query_grad, key_grad, value_grad = kernel_call(
        finish_body,
        (narrow, narrow, narrow),
        4,
        (moved, grad_far, value_far, key_far),
        [near] + [far] * 3,
        [local] * 3 + [pltpu.SemaphoreType.DMA((3,))],
    )
    filter_grad = kernel_call(add_body, line, 4, (partial, swapped), [near, near]).reshape(width)
    return (query_grad, key_grad, value_grad, filter_grad)


def solution(mesh):
    placed = (P("ch", "ctx"), P("ch", "ctx"), P("ch", "ctx"), P("ctx"), P("ch", "ctx"))
    return jax.shard_map(
        shards,
        mesh=mesh,
        in_specs=placed,
        out_specs=(P("ch", "ctx"), P("ch", "ctx"), P("ch", "ctx"), P("ctx")),
        check_vma=False,
    )
```

```python
import math

import jax
import jax.numpy as jnp
import numpy as np
from jax import lax
from jax.experimental import pallas as pl
from jax.experimental.pallas import tpu as pltpu
from jax.sharding import PartitionSpec as P

SHIFT = 0.25
MIB = 1024 * 1024
ORDER = np.roll(np.arange(64), -((1 * 8 + 4) * 4 + 2))
AHEAD, BACK, TWIST = 4, 8, 9


def halves(values):
    high = values.astype(jnp.bfloat16)
    low = (values - np.asarray(high).astype(np.float64)).astype(jnp.bfloat16)
    return np.asarray(high), np.asarray(low)


def table_bank(blocks, width):
    length = blocks * width
    half = width // 2
    rows = np.arange(blocks) + SHIFT
    planes = []
    for odd in (0, 1):
        angle = 2.0 * math.pi * (np.outer(np.arange(half), 2 * np.arange(half) + odd) % width) / width
        cosine, sine = np.cos(angle), np.sin(angle)
        planes += halves(np.block([[cosine, -sine], [sine, cosine]]))
    block_angle = 2.0 * math.pi * np.outer(rows, np.arange(blocks)) / blocks
    block_table = np.concatenate([np.cos(block_angle), -np.sin(block_angle)], axis=0)
    own = [2 * ORDER + parity for parity in (0, 1)]
    for e in (0, 1):
        high, low = halves(np.concatenate([block_table[:, own[e]], block_table[:, own[1 - e]]], axis=1))
        planes += [np.concatenate([high, high], axis=1), np.concatenate([low, np.zeros_like(low)], axis=1)]
    pieces = [np.concatenate(halves(block_table.T[own[e]] / length), axis=0) for e in (0, 1)]
    planes.append(np.concatenate(pieces, axis=0))
    twist_angle = 2.0 * math.pi * np.outer(rows, np.arange(width)) / length
    planes += [np.concatenate(halves(np.cos(twist_angle)), axis=0), np.concatenate(halves(np.sin(twist_angle)), axis=0)]
    return np.stack(planes)


def split(values):
    high = values.astype(jnp.bfloat16)
    return high, (values - high.astype(jnp.float32)).astype(jnp.bfloat16)


def product(left, right, transposed=False):
    contracted = (((1,), (1 if transposed else 0,)), ((), ()))
    return lax.dot_general(left, right, contracted, preferred_element_type=jnp.float32)


def inner_product(values, bank_ref, odd, transposed):
    count = values.shape[0]
    high, low = split(values)
    wide = product(jnp.concatenate([high, low], axis=0), bank_ref[2 * odd], transposed)
    return wide[:count] + wide[count:] + product(high, bank_ref[2 * odd + 1], transposed)


def fetch(pairs, arrived):
    copies = [pltpu.make_async_copy(source, here, arrived.at[i]) for i, (source, here) in enumerate(pairs)]
    for copy in copies:
        copy.start()
    return copies


def pack_body(key_far, value_far, grad_far, query_far, taps_far, out_ref, key, value, grad, query, taps, arrived):
    width = key.shape[1]
    copies = fetch(
        ((key_far, key), (value_far, value), (grad_far, grad), (query_far, query), (taps_far, taps)), arrived
    )
    copies[0].wait()
    copies[1].wait()
    out_ref[:, 0, :width] = key[...].astype(jnp.float32) * value[...].astype(jnp.float32)
    copies[2].wait()
    copies[3].wait()
    out_ref[:, 0, width : 2 * width] = grad[...].astype(jnp.float32) * query[...].astype(jnp.float32)
    copies[4].wait()
    out_ref[:, 0, 2 * width :] = jnp.broadcast_to(taps[...], key.shape)


def lead_body(own_ref, bank_far, bank_ref, arrived):
    for copy in fetch([(bank_far, bank_ref)], arrived):
        copy.wait()


def middle_body(scale, parity_ref, own_ref, other_ref, bank_ref, out_ref):
    parity = parity_ref[0]
    width = bank_ref.shape[2]
    half = width // 2
    rows = 2 * own_ref.shape[0]
    ahead = bank_ref[pl.ds(AHEAD + 2 * parity, 2)].reshape(2 * width, width)
    signal = jnp.concatenate([own_ref[:, 0, :], other_ref[:, 0, :]], axis=0)
    front = product(ahead, jnp.concatenate(split(signal), axis=0))
    front = front[: 2 * rows] + front[2 * rows :]
    twist = [bank_ref[TWIST + i].astype(jnp.float32) for i in (0, 1)]
    cosine, sine = [table[:rows] + table[rows:] for table in twist]
    even, odd = [], []
    for index in range(3):
        real = front[:rows, index * width : (index + 1) * width]
        imag = front[rows:, index * width : (index + 1) * width]
        real, imag = real * cosine + imag * sine, imag * cosine - real * sine
        even.append(jnp.concatenate([real[:, :half] + real[:, half:], imag[:, :half] + imag[:, half:]], axis=1))
        odd.append(jnp.concatenate([real[:, :half] - real[:, half:], imag[:, :half] - imag[:, half:]], axis=1))
    waves = []
    for bins, stacked in enumerate((even, odd)):
        spectra = inner_product(jnp.concatenate(stacked, axis=0), bank_ref, bins, False)
        gated_real, gated_imag = spectra[:rows, :half], spectra[:rows, half:]
        grad_real, grad_imag = spectra[rows : 2 * rows, :half], spectra[rows : 2 * rows, half:]
        taps_real, taps_imag = spectra[2 * rows :, :half], spectra[2 * rows :, half:]
        conv_real = gated_real * taps_real - gated_imag * taps_imag
        conv_imag = gated_real * taps_imag + gated_imag * taps_real
        back_real = grad_real * taps_real + grad_imag * taps_imag
        back_imag = grad_imag * taps_real - grad_real * taps_imag
        cross_real = (grad_real * gated_real + grad_imag * gated_imag) * scale
        cross_imag = (grad_imag * gated_real - grad_real * gated_imag) * scale
        mixed = jnp.concatenate(
            [
                jnp.concatenate([conv_real, conv_imag], axis=1),
                jnp.concatenate([back_real, back_imag], axis=1),
                jnp.concatenate([cross_real, cross_imag], axis=1),
            ],
            axis=0,
        )
        waves.append(inner_product(mixed, bank_ref, bins, True))
    turned = []
    for index in range(3):
        first = waves[0][index * rows : (index + 1) * rows]
        second = waves[1][index * rows : (index + 1) * rows]
        total, difference = first + second, first - second
        real = jnp.concatenate([total[:, :half], difference[:, :half]], axis=1)
        imag = jnp.concatenate([total[:, half:], difference[:, half:]], axis=1)
        turned.append(jnp.concatenate([real * cosine - imag * sine, real * sine + imag * cosine], axis=0))
    high, low = split(jnp.concatenate(turned, axis=1))
    table = bank_ref[BACK, pl.ds(pl.multiple_of(rows * parity, rows), rows)]
    wide = product(table, high)
    out_ref[:, 0, :] = wide[: rows // 2] + wide[rows // 2 :] + product(table[: rows // 2], low)


def sum_body(moved_ref, out_ref):
    width = out_ref.shape[1]
    out_ref[...] = jnp.sum(moved_ref[:, 0, 2 * width :], axis=0, keepdims=True)


def finish_body(moved_ref, grad_far, value_far, key_far, query_out, key_out, value_out, grad, value, key, arrived):
    width = key.shape[1]
    copies = fetch(((grad_far, grad), (value_far, value), (key_far, key)), arrived)
    back = moved_ref[:, 0, width : 2 * width]
    copies[0].wait()
    query_out[...] = (grad[...].astype(jnp.float32) * moved_ref[:, 0, :width]).astype(jnp.bfloat16)
    copies[1].wait()
    key_out[...] = (back * value[...].astype(jnp.float32)).astype(jnp.bfloat16)
    copies[2].wait()
    value_out[...] = (back * key[...].astype(jnp.float32)).astype(jnp.bfloat16)


def add_body(left_ref, right_ref, out_ref):
    out_ref[...] = left_ref[...] + right_ref[...]


def kernel_call(body, out_shape, limit, operands, in_specs, scratch=()):
    return pl.pallas_call(
        body,
        out_shape=out_shape,
        in_specs=in_specs,
        scratch_shapes=scratch,
        compiler_params=pltpu.CompilerParams(vmem_limit_bytes=limit * MIB),
    )(*operands)


def shards(query_proj, key_proj, value_proj, filter_taps, out_grad):
    devices = lax.axis_size("ctx")
    channels, width = query_proj.shape
    chips = devices // 2
    parity = (lax.axis_index("ctx") % 2).astype(jnp.int32).reshape(1)
    same_core = [[int(2 * chip + core) for chip in ORDER] for core in (0, 1)]
    other_core = [(device, device ^ 1) for device in range(devices)]
    scale = 1.0 / math.sqrt(channels * lax.axis_size("ch") * devices * width)
    message = jax.ShapeDtypeStruct((chips, 1, 3 * width), jnp.float32)
    narrow = jax.ShapeDtypeStruct((channels, width), jnp.bfloat16)
    bank = jnp.asarray(table_bank(devices, width))

    def exchange(array):
        return lax.all_to_all(array, "ctx", 0, 0, axis_index_groups=same_core, tiled=True)

    def middle(*refs):
        middle_body(scale, *refs)

    far = pl.BlockSpec(memory_space=pltpu.HBM)
    key_far, value_far, grad_far, query_far, taps_far = [
        pltpu.with_memory_space_constraint(array, pltpu.HBM)
        for array in (key_proj, value_proj, out_grad, query_proj, filter_taps.reshape(1, width))
    ]
    near = pl.BlockSpec(memory_space=pltpu.VMEM)
    scalar = pl.BlockSpec(memory_space=pltpu.SMEM)
    local = pltpu.VMEM((channels, width), jnp.bfloat16)
    packed = kernel_call(
        pack_body,
        message,
        4,
        (key_far, value_far, grad_far, query_far, taps_far),
        [far] * 5,
        [local] * 4 + [pltpu.VMEM((1, width), jnp.float32), pltpu.SemaphoreType.DMA((5,))],
    )
    own = exchange(packed)
    other = lax.ppermute(own, "ctx", other_core)
    near_bank = kernel_call(
        lead_body,
        jax.ShapeDtypeStruct(bank.shape, bank.dtype),
        8,
        (own, pltpu.with_memory_space_constraint(bank, pltpu.HBM)),
        [near, far],
        [pltpu.SemaphoreType.DMA((1,))],
    )
    restored = kernel_call(middle, message, 24, (parity, own, other, near_bank), [scalar, near, near, near])
    moved = exchange(restored)
    line = jax.ShapeDtypeStruct((1, width), jnp.float32)
    partial = kernel_call(sum_body, line, 4, (moved,), [near])
    swapped = lax.ppermute(partial, "ch", [(0, 1), (1, 0)])
    query_grad, key_grad, value_grad = kernel_call(
        finish_body,
        (narrow, narrow, narrow),
        4,
        (moved, grad_far, value_far, key_far),
        [near] + [far] * 3,
        [local] * 3 + [pltpu.SemaphoreType.DMA((3,))],
    )
    filter_grad = kernel_call(add_body, line, 4, (partial, swapped), [near, near]).reshape(width)
    return (query_grad, key_grad, value_grad, filter_grad)


def solution(mesh):
    placed = (P("ch", "ctx"), P("ch", "ctx"), P("ch", "ctx"), P("ctx"), P("ch", "ctx"))
    return jax.shard_map(
        shards,
        mesh=mesh,
        in_specs=placed,
        out_specs=(P("ch", "ctx"), P("ch", "ctx"), P("ch", "ctx"), P("ctx")),
        check_vma=False,
    )
```

```python
import math

import jax
import jax.numpy as jnp
import numpy as np
from jax import lax
from jax.experimental import pallas as pl
from jax.experimental.pallas import tpu as pltpu
from jax.sharding import PartitionSpec as P

SHIFT = 0.25
MIB = 1024 * 1024
ORDER = np.array([((1 - x) * 8 + (4 + 3 * z) % 8) * 4 + (2 + y) % 4 for z in range(8) for y in range(4) for x in range(2)])
AHEAD, BACK, TWIST = 4, 8, 9


def halves(values):
    high = values.astype(jnp.bfloat16)
    low = (values - np.asarray(high).astype(np.float64)).astype(jnp.bfloat16)
    return np.asarray(high), np.asarray(low)


def table_bank(blocks, width):
    length = blocks * width
    half = width // 2
    rows = np.arange(blocks) + SHIFT
    planes = []
    for odd in (0, 1):
        angle = 2.0 * math.pi * (np.outer(np.arange(half), 2 * np.arange(half) + odd) % width) / width
        cosine, sine = np.cos(angle), np.sin(angle)
        planes += halves(np.block([[cosine, -sine], [sine, cosine]]))
    block_angle = 2.0 * math.pi * np.outer(rows, np.arange(blocks)) / blocks
    block_table = np.concatenate([np.cos(block_angle), -np.sin(block_angle)], axis=0)
    own = [2 * ORDER + parity for parity in (0, 1)]
    for e in (0, 1):
        high, low = halves(np.concatenate([block_table[:, own[e]], block_table[:, own[1 - e]]], axis=1))
        planes += [np.concatenate([high, high], axis=1), np.concatenate([low, np.zeros_like(low)], axis=1)]
    pieces = [np.concatenate(halves(block_table.T[own[e]] / length), axis=0) for e in (0, 1)]
    planes.append(np.concatenate(pieces, axis=0))
    twist_angle = 2.0 * math.pi * np.outer(rows, np.arange(width)) / length
    planes += [np.concatenate(halves(np.cos(twist_angle)), axis=0), np.concatenate(halves(np.sin(twist_angle)), axis=0)]
    return np.stack(planes)


def split(values):
    high = values.astype(jnp.bfloat16)
    return high, (values - high.astype(jnp.float32)).astype(jnp.bfloat16)


def product(left, right, transposed=False):
    contracted = (((1,), (1 if transposed else 0,)), ((), ()))
    return lax.dot_general(left, right, contracted, preferred_element_type=jnp.float32)


def inner_product(values, bank_ref, odd, transposed):
    count = values.shape[0]
    high, low = split(values)
    wide = product(jnp.concatenate([high, low], axis=0), bank_ref[2 * odd], transposed)
    return wide[:count] + wide[count:] + product(high, bank_ref[2 * odd + 1], transposed)


def fetch(pairs, arrived):
    copies = [pltpu.make_async_copy(source, here, arrived.at[i]) for i, (source, here) in enumerate(pairs)]
    for copy in copies:
        copy.start()
    return copies


def pack_body(key_far, value_far, grad_far, query_far, taps_far, out_ref, key, value, grad, query, taps, arrived):
    width = key.shape[1]
    copies = fetch(
        ((key_far, key), (value_far, value), (grad_far, grad), (query_far, query), (taps_far, taps)), arrived
    )
    copies[0].wait()
    copies[1].wait()
    out_ref[:, 0, :width] = key[...].astype(jnp.float32) * value[...].astype(jnp.float32)
    copies[2].wait()
    copies[3].wait()
    out_ref[:, 0, width : 2 * width] = grad[...].astype(jnp.float32) * query[...].astype(jnp.float32)
    copies[4].wait()
    out_ref[:, 0, 2 * width :] = jnp.broadcast_to(taps[...], key.shape)


def lead_body(own_ref, bank_far, bank_ref, arrived):
    for copy in fetch([(bank_far, bank_ref)], arrived):
        copy.wait()


def middle_body(scale, parity_ref, own_ref, other_ref, bank_ref, out_ref):
    parity = parity_ref[0]
    width = bank_ref.shape[2]
    half = width // 2
    rows = 2 * own_ref.shape[0]
    ahead = bank_ref[pl.ds(AHEAD + 2 * parity, 2)].reshape(2 * width, width)
    signal = jnp.concatenate([own_ref[:, 0, :], other_ref[:, 0, :]], axis=0)
    front = product(ahead, jnp.concatenate(split(signal), axis=0))
    front = front[: 2 * rows] + front[2 * rows :]
    twist = [bank_ref[TWIST + i].astype(jnp.float32) for i in (0, 1)]
    cosine, sine = [table[:rows] + table[rows:] for table in twist]
    even, odd = [], []
    for index in range(3):
        real = front[:rows, index * width : (index + 1) * width]
        imag = front[rows:, index * width : (index + 1) * width]
        real, imag = real * cosine + imag * sine, imag * cosine - real * sine
        even.append(jnp.concatenate([real[:, :half] + real[:, half:], imag[:, :half] + imag[:, half:]], axis=1))
        odd.append(jnp.concatenate([real[:, :half] - real[:, half:], imag[:, :half] - imag[:, half:]], axis=1))
    waves = []
    for bins, stacked in enumerate((even, odd)):
        spectra = inner_product(jnp.concatenate(stacked, axis=0), bank_ref, bins, False)
        gated_real, gated_imag = spectra[:rows, :half], spectra[:rows, half:]
        grad_real, grad_imag = spectra[rows : 2 * rows, :half], spectra[rows : 2 * rows, half:]
        taps_real, taps_imag = spectra[2 * rows :, :half], spectra[2 * rows :, half:]
        conv_real = gated_real * taps_real - gated_imag * taps_imag
        conv_imag = gated_real * taps_imag + gated_imag * taps_real
        back_real = grad_real * taps_real + grad_imag * taps_imag
        back_imag = grad_imag * taps_real - grad_real * taps_imag
        cross_real = (grad_real * gated_real + grad_imag * gated_imag) * scale
        cross_imag = (grad_imag * gated_real - grad_real * gated_imag) * scale
        mixed = jnp.concatenate(
            [
                jnp.concatenate([conv_real, conv_imag], axis=1),
                jnp.concatenate([back_real, back_imag], axis=1),
                jnp.concatenate([cross_real, cross_imag], axis=1),
            ],
            axis=0,
        )
        waves.append(inner_product(mixed, bank_ref, bins, True))
    turned = []
    for index in range(3):
        first = waves[0][index * rows : (index + 1) * rows]
        second = waves[1][index * rows : (index + 1) * rows]
        total, difference = first + second, first - second
        real = jnp.concatenate([total[:, :half], difference[:, :half]], axis=1)
        imag = jnp.concatenate([total[:, half:], difference[:, half:]], axis=1)
        turned.append(jnp.concatenate([real * cosine - imag * sine, real * sine + imag * cosine], axis=0))
    high, low = split(jnp.concatenate(turned, axis=1))
    table = bank_ref[BACK, pl.ds(pl.multiple_of(rows * parity, rows), rows)]
    wide = product(table, high)
    out_ref[:, 0, :] = wide[: rows // 2] + wide[rows // 2 :] + product(table[: rows // 2], low)


def sum_body(moved_ref, out_ref):
    width = out_ref.shape[1]
    out_ref[...] = jnp.sum(moved_ref[:, 0, 2 * width :], axis=0, keepdims=True)


def finish_body(moved_ref, key_ref, value_ref, grad_ref, query_out, key_out, value_out):
    width = key_ref.shape[1]
    back = moved_ref[:, 0, width : 2 * width]
    query_out[...] = (grad_ref[...].astype(jnp.float32) * moved_ref[:, 0, :width]).astype(jnp.bfloat16)
    key_out[...] = (back * value_ref[...].astype(jnp.float32)).astype(jnp.bfloat16)
    value_out[...] = (back * key_ref[...].astype(jnp.float32)).astype(jnp.bfloat16)


def add_body(left_ref, right_ref, out_ref):
    out_ref[...] = left_ref[...] + right_ref[...]


def kernel_call(body, out_shape, limit, operands, in_specs, scratch=()):
    return pl.pallas_call(
        body,
        out_shape=out_shape,
        in_specs=in_specs,
        scratch_shapes=scratch,
        compiler_params=pltpu.CompilerParams(vmem_limit_bytes=limit * MIB),
    )(*operands)


def shards(query_proj, key_proj, value_proj, filter_taps, out_grad):
    devices = lax.axis_size("ctx")
    channels, width = query_proj.shape
    chips = devices // 2
    parity = (lax.axis_index("ctx") % 2).astype(jnp.int32).reshape(1)
    same_core = [[int(2 * chip + core) for chip in ORDER] for core in (0, 1)]
    other_core = [(device, device ^ 1) for device in range(devices)]
    scale = 1.0 / math.sqrt(channels * lax.axis_size("ch") * devices * width)
    message = jax.ShapeDtypeStruct((chips, 1, 3 * width), jnp.float32)
    narrow = jax.ShapeDtypeStruct((channels, width), jnp.bfloat16)
    bank = jnp.asarray(table_bank(devices, width))

    def exchange(array):
        return lax.all_to_all(array, "ctx", 0, 0, axis_index_groups=same_core, tiled=True)

    def middle(*refs):
        middle_body(scale, *refs)

    far = pl.BlockSpec(memory_space=pltpu.HBM)
    key_far, value_far, grad_far, query_far, taps_far = [
        pltpu.with_memory_space_constraint(array, pltpu.HBM)
        for array in (key_proj, value_proj, out_grad, query_proj, filter_taps.reshape(1, width))
    ]
    near = pl.BlockSpec(memory_space=pltpu.VMEM)
    scalar = pl.BlockSpec(memory_space=pltpu.SMEM)
    local = pltpu.VMEM((channels, width), jnp.bfloat16)
    packed, key, value, grad = kernel_call(
        pack_body,
        (message, narrow, narrow, narrow),
        4,
        (key_far, value_far, grad_far, query_far, taps_far),
        [far] * 5,
        [local, pltpu.VMEM((1, width), jnp.float32), pltpu.SemaphoreType.DMA((5,))],
    )
    own = exchange(packed)
    other = lax.ppermute(own, "ctx", other_core)
    near_bank = kernel_call(
        lead_body,
        jax.ShapeDtypeStruct(bank.shape, bank.dtype),
        8,
        (own, pltpu.with_memory_space_constraint(bank, pltpu.HBM)),
        [near, far],
        [pltpu.SemaphoreType.DMA((1,))],
    )
    restored = kernel_call(middle, message, 24, (parity, own, other, near_bank), [scalar, near, near, near])
    moved = exchange(restored)
    line = jax.ShapeDtypeStruct((1, width), jnp.float32)
    partial = kernel_call(sum_body, line, 4, (moved,), [near])
    swapped = lax.ppermute(partial, "ch", [(0, 1), (1, 0)])
    query_grad, key_grad, value_grad = kernel_call(
        finish_body, (narrow, narrow, narrow), 4, (moved, key, value, grad), [near] * 4
    )
    filter_grad = kernel_call(add_body, line, 4, (partial, swapped), [near, near]).reshape(width)
    return (query_grad, key_grad, value_grad, filter_grad)


def solution(mesh):
    placed = (P("ch", "ctx"), P("ch", "ctx"), P("ch", "ctx"), P("ctx"), P("ch", "ctx"))
    return jax.shard_map(
        shards,
        mesh=mesh,
        in_specs=placed,
        out_specs=(P("ch", "ctx"), P("ch", "ctx"), P("ch", "ctx"), P("ctx")),
        check_vma=False,
    )
```

```python
import math

import jax
import jax.numpy as jnp
import numpy as np
from jax import lax
from jax.experimental import pallas as pl
from jax.experimental.pallas import tpu as pltpu
from jax.sharding import PartitionSpec as P

SHIFT = 0.25
MIB = 1024 * 1024
PARTS = 2
ORDER = np.array([((1 - x) * 8 + (4 + 3 * z) % 8) * 4 + (2 + y) % 4 for z in range(8) for y in range(4) for x in range(2)])
AHEAD, BACK, TWIST = 4, 8, 9


def halves(values):
    high = values.astype(jnp.bfloat16)
    low = (values - np.asarray(high).astype(np.float64)).astype(jnp.bfloat16)
    return np.asarray(high), np.asarray(low)


def table_bank(blocks, width):
    length = blocks * width
    half = width // 2
    rows = np.arange(blocks) + SHIFT
    planes = []
    for odd in (0, 1):
        angle = 2.0 * math.pi * (np.outer(np.arange(half), 2 * np.arange(half) + odd) % width) / width
        cosine, sine = np.cos(angle), np.sin(angle)
        planes += halves(np.block([[cosine, -sine], [sine, cosine]]))
    block_angle = 2.0 * math.pi * np.outer(rows, np.arange(blocks)) / blocks
    block_table = np.concatenate([np.cos(block_angle), -np.sin(block_angle)], axis=0)
    own = [2 * ORDER + parity for parity in (0, 1)]
    for e in (0, 1):
        high, low = halves(np.concatenate([block_table[:, own[e]], block_table[:, own[1 - e]]], axis=1))
        planes += [np.concatenate([high, high], axis=1), np.concatenate([low, np.zeros_like(low)], axis=1)]
    pieces = [np.concatenate(halves(block_table.T[own[e]] / length), axis=0) for e in (0, 1)]
    planes.append(np.concatenate(pieces, axis=0))
    twist_angle = 2.0 * math.pi * np.outer(rows, np.arange(width)) / length
    planes += [np.concatenate(halves(np.cos(twist_angle)), axis=0), np.concatenate(halves(np.sin(twist_angle)), axis=0)]
    return np.stack(planes)


def split(values):
    high = values.astype(jnp.bfloat16)
    return high, (values - high.astype(jnp.float32)).astype(jnp.bfloat16)


def product(left, right, transposed=False):
    contracted = (((1,), (1 if transposed else 0,)), ((), ()))
    return lax.dot_general(left, right, contracted, preferred_element_type=jnp.float32)


def inner_product(values, bank_ref, odd, transposed):
    count = values.shape[0]
    high, low = split(values)
    wide = product(jnp.concatenate([high, low], axis=0), bank_ref[2 * odd], transposed)
    return wide[:count] + wide[count:] + product(high, bank_ref[2 * odd + 1], transposed)


def fetch(pairs, arrived):
    copies = [pltpu.make_async_copy(source, here, arrived.at[i]) for i, (source, here) in enumerate(pairs)]
    for copy in copies:
        copy.start()
    return copies


def pack_body(key_far, value_far, grad_far, query_far, taps_far, out_ref, key, value, grad, query, taps, arrived):
    width = key.shape[1]
    copies = fetch(
        ((key_far, key), (value_far, value), (grad_far, grad), (query_far, query), (taps_far, taps)), arrived
    )
    copies[0].wait()
    copies[1].wait()
    out_ref[:, 0, :width] = key[...].astype(jnp.float32) * value[...].astype(jnp.float32)
    copies[2].wait()
    copies[3].wait()
    out_ref[:, 0, width : 2 * width] = grad[...].astype(jnp.float32) * query[...].astype(jnp.float32)
    copies[4].wait()
    out_ref[:, 0, 2 * width :] = jnp.broadcast_to(taps[...], key.shape)


def lead_body(own_ref, bank_far, bank_ref, arrived):
    for copy in fetch([(bank_far, bank_ref)], arrived):
        copy.wait()


def middle_body(scale, parity_ref, own_ref, other_ref, bank_ref, out_ref):
    parity = parity_ref[0]
    width = bank_ref.shape[2]
    half = width // 2
    rows = 2 * own_ref.shape[0]
    ahead = bank_ref[pl.ds(AHEAD + 2 * parity, 2)].reshape(2 * width, width)
    signal = jnp.concatenate([own_ref[:, 0, :], other_ref[:, 0, :]], axis=0)
    data = jnp.concatenate(split(signal), axis=0)
    fronts = []
    for index in range(3):
        wide = product(ahead, data[:, index * width : (index + 1) * width])
        fronts.append(wide[: 2 * rows] + wide[2 * rows :])
    twist = [bank_ref[TWIST + i].astype(jnp.float32) for i in (0, 1)]
    cosine, sine = [table[:rows] + table[rows:] for table in twist]
    reals = [[] for _ in range(3)]
    imags = [[] for _ in range(3)]
    size = rows // PARTS
    stacks, spectras, mixes, outs = {}, {}, {}, {}
    pieces = [(part, bins) for bins in (0, 1) for part in range(PARTS)]

    def twisted(part):
        here = slice(part * size, (part + 1) * size)
        there = slice(rows + part * size, rows + (part + 1) * size)
        even, odd = [], []
        for index in range(3):
            real = fronts[index][here]
            imag = fronts[index][there]
            real, imag = real * cosine[here] + imag * sine[here], imag * cosine[here] - real * sine[here]
            even.append(jnp.concatenate([real[:, :half] + real[:, half:], imag[:, :half] + imag[:, half:]], axis=1))
            odd.append(jnp.concatenate([real[:, :half] - real[:, half:], imag[:, :half] - imag[:, half:]], axis=1))
        stacks[part, 0] = jnp.concatenate(even, axis=0)
        stacks[part, 1] = jnp.concatenate(odd, axis=0)

    def mix(key):
        spectra = spectras[key]
        gated_real, gated_imag = spectra[:size, :half], spectra[:size, half:]
        grad_real, grad_imag = spectra[size : 2 * size, :half], spectra[size : 2 * size, half:]
        taps_real, taps_imag = spectra[2 * size :, :half], spectra[2 * size :, half:]
        conv_real = gated_real * taps_real - gated_imag * taps_imag
        conv_imag = gated_real * taps_imag + gated_imag * taps_real
        back_real = grad_real * taps_real + grad_imag * taps_imag
        back_imag = grad_imag * taps_real - grad_real * taps_imag
        cross_real = (grad_real * gated_real + grad_imag * gated_imag) * scale
        cross_imag = (grad_imag * gated_real - grad_real * gated_imag) * scale
        mixes[key] = jnp.concatenate(
            [
                jnp.concatenate([conv_real, conv_imag], axis=1),
                jnp.concatenate([back_real, back_imag], axis=1),
                jnp.concatenate([cross_real, cross_imag], axis=1),
            ],
            axis=0,
        )

    def untwist(part):
        here = slice(part * size, (part + 1) * size)
        for index in range(3):
            first = outs[part, 0][index * size : (index + 1) * size]
            second = outs[part, 1][index * size : (index + 1) * size]
            total, difference = first + second, first - second
            real = jnp.concatenate([total[:, :half], difference[:, :half]], axis=1)
            imag = jnp.concatenate([total[:, half:], difference[:, half:]], axis=1)
            reals[index].append(real * cosine[here] - imag * sine[here])
            imags[index].append(real * sine[here] + imag * cosine[here])

    for part in range(PARTS):
        twisted(part)
    for key in pieces:
        spectras[key] = inner_product(stacks[key], bank_ref, key[1], False)
    for key in pieces:
        mix(key)
    for key in pieces:
        outs[key] = inner_product(mixes[key], bank_ref, key[1], True)
    for part in range(PARTS):
        untwist(part)
    table = bank_ref[BACK, pl.ds(pl.multiple_of(rows * parity, rows), rows)]
    for index in range(3):
        high, low = split(jnp.concatenate(reals[index] + imags[index], axis=0))
        wide = product(table, high)
        out_ref[:, 0, index * width : (index + 1) * width] = (
            wide[: rows // 2] + wide[rows // 2 :] + product(table[: rows // 2], low)
        )


def sum_body(moved_ref, out_ref):
    width = out_ref.shape[1]
    out_ref[...] = jnp.sum(moved_ref[:, 0, 2 * width :], axis=0, keepdims=True)


def finish_body(moved_ref, key_ref, value_ref, grad_ref, query_out, key_out, value_out):
    width = key_ref.shape[1]
    back = moved_ref[:, 0, width : 2 * width]
    query_out[...] = (grad_ref[...].astype(jnp.float32) * moved_ref[:, 0, :width]).astype(jnp.bfloat16)
    key_out[...] = (back * value_ref[...].astype(jnp.float32)).astype(jnp.bfloat16)
    value_out[...] = (back * key_ref[...].astype(jnp.float32)).astype(jnp.bfloat16)


def add_body(left_ref, right_ref, out_ref):
    out_ref[...] = left_ref[...] + right_ref[...]


def kernel_call(body, out_shape, limit, operands, in_specs, scratch=()):
    return pl.pallas_call(
        body,
        out_shape=out_shape,
        in_specs=in_specs,
        scratch_shapes=scratch,
        compiler_params=pltpu.CompilerParams(vmem_limit_bytes=limit * MIB),
    )(*operands)


def shards(query_proj, key_proj, value_proj, filter_taps, out_grad):
    devices = lax.axis_size("ctx")
    channels, width = query_proj.shape
    chips = devices // 2
    parity = (lax.axis_index("ctx") % 2).astype(jnp.int32).reshape(1)
    same_core = [[int(2 * chip + core) for chip in ORDER] for core in (0, 1)]
    other_core = [(device, device ^ 1) for device in range(devices)]
    scale = 1.0 / math.sqrt(channels * lax.axis_size("ch") * devices * width)
    message = jax.ShapeDtypeStruct((chips, 1, 3 * width), jnp.float32)
    narrow = jax.ShapeDtypeStruct((channels, width), jnp.bfloat16)
    bank = jnp.asarray(table_bank(devices, width))

    def exchange(array):
        return lax.all_to_all(array, "ctx", 0, 0, axis_index_groups=same_core, tiled=True)

    def middle(*refs):
        middle_body(scale, *refs)

    far = pl.BlockSpec(memory_space=pltpu.HBM)
    key_far, value_far, grad_far, query_far, taps_far = [
        pltpu.with_memory_space_constraint(array, pltpu.HBM)
        for array in (key_proj, value_proj, out_grad, query_proj, filter_taps.reshape(1, width))
    ]
    near = pl.BlockSpec(memory_space=pltpu.VMEM)
    scalar = pl.BlockSpec(memory_space=pltpu.SMEM)
    local = pltpu.VMEM((channels, width), jnp.bfloat16)
    packed, key, value, grad = kernel_call(
        pack_body,
        (message, narrow, narrow, narrow),
        4,
        (key_far, value_far, grad_far, query_far, taps_far),
        [far] * 5,
        [local, pltpu.VMEM((1, width), jnp.float32), pltpu.SemaphoreType.DMA((5,))],
    )
    own = exchange(packed)
    other = lax.ppermute(own, "ctx", other_core)
    near_bank = kernel_call(
        lead_body,
        jax.ShapeDtypeStruct(bank.shape, bank.dtype),
        8,
        (own, pltpu.with_memory_space_constraint(bank, pltpu.HBM)),
        [near, far],
        [pltpu.SemaphoreType.DMA((1,))],
    )
    restored = kernel_call(middle, message, 24, (parity, own, other, near_bank), [scalar, near, near, near])
    moved = exchange(restored)
    line = jax.ShapeDtypeStruct((1, width), jnp.float32)
    partial = kernel_call(sum_body, line, 4, (moved,), [near])
    swapped = lax.ppermute(partial, "ch", [(0, 1), (1, 0)])
    query_grad, key_grad, value_grad = kernel_call(
        finish_body, (narrow, narrow, narrow), 4, (moved, key, value, grad), [near] * 4
    )
    filter_grad = kernel_call(add_body, line, 4, (partial, swapped), [near, near]).reshape(width)
    return (query_grad, key_grad, value_grad, filter_grad)


def solution(mesh):
    placed = (P("ch", "ctx"), P("ch", "ctx"), P("ch", "ctx"), P("ctx"), P("ch", "ctx"))
    return jax.shard_map(
        shards,
        mesh=mesh,
        in_specs=placed,
        out_specs=(P("ch", "ctx"), P("ch", "ctx"), P("ch", "ctx"), P("ctx")),
        check_vma=False,
    )
```

```python
import math

import jax
import jax.numpy as jnp
import numpy as np
from jax import lax
from jax.experimental import pallas as pl
from jax.experimental.pallas import tpu as pltpu
from jax.sharding import PartitionSpec as P

SHIFT = 0.25
MIB = 1024 * 1024
PARTS = 2
ORDER = np.array([((1 - x) * 8 + (4 + 3 * z) % 8) * 4 + (2 + y) % 4 for z in range(8) for y in range(4) for x in range(2)])
AHEAD, BACK, TWIST = 4, 8, 9


def halves(values):
    high = values.astype(jnp.bfloat16)
    low = (values - np.asarray(high).astype(np.float64)).astype(jnp.bfloat16)
    return np.asarray(high), np.asarray(low)


def table_bank(blocks, width):
    length = blocks * width
    half = width // 2
    rows = np.arange(blocks) + SHIFT
    planes = []
    for odd in (0, 1):
        angle = 2.0 * math.pi * (np.outer(np.arange(half), 2 * np.arange(half) + odd) % width) / width
        cosine, sine = np.cos(angle), np.sin(angle)
        planes += halves(np.block([[cosine, -sine], [sine, cosine]]))
    block_angle = 2.0 * math.pi * np.outer(rows, np.arange(blocks)) / blocks
    block_table = np.concatenate([np.cos(block_angle), -np.sin(block_angle)], axis=0)
    own = [2 * ORDER + parity for parity in (0, 1)]
    for e in (0, 1):
        high, low = halves(np.concatenate([block_table[:, own[e]], block_table[:, own[1 - e]]], axis=1))
        planes += [np.concatenate([high, high], axis=1), np.concatenate([low, np.zeros_like(low)], axis=1)]
    pieces = [np.concatenate(halves(block_table.T[own[e]] / length), axis=0) for e in (0, 1)]
    planes.append(np.concatenate(pieces, axis=0))
    twist_angle = 2.0 * math.pi * np.outer(rows, np.arange(width)) / length
    planes += [np.concatenate(halves(np.cos(twist_angle)), axis=0), np.concatenate(halves(np.sin(twist_angle)), axis=0)]
    return np.stack(planes)


def split(values):
    high = values.astype(jnp.bfloat16)
    return high, (values - high.astype(jnp.float32)).astype(jnp.bfloat16)


def product(left, right, transposed=False):
    contracted = (((1,), (1 if transposed else 0,)), ((), ()))
    return lax.dot_general(left, right, contracted, preferred_element_type=jnp.float32)


def inner_product(values, bank_ref, odd, transposed):
    count = values.shape[0]
    high, low = split(values)
    wide = product(jnp.concatenate([high, low], axis=0), bank_ref[2 * odd], transposed)
    return wide[:count] + wide[count:] + product(high, bank_ref[2 * odd + 1], transposed)


def fetch(pairs, arrived):
    copies = [pltpu.make_async_copy(source, here, arrived.at[i]) for i, (source, here) in enumerate(pairs)]
    for copy in copies:
        copy.start()
    return copies


def pack_body(key_far, value_far, grad_far, query_far, taps_far, out_ref, key, value, grad, query, taps, arrived):
    width = key.shape[1]
    copies = fetch(
        ((key_far, key), (value_far, value), (grad_far, grad), (query_far, query), (taps_far, taps)), arrived
    )
    copies[0].wait()
    copies[1].wait()
    out_ref[:, 0, :width] = key[...].astype(jnp.float32) * value[...].astype(jnp.float32)
    copies[2].wait()
    copies[3].wait()
    out_ref[:, 0, width : 2 * width] = grad[...].astype(jnp.float32) * query[...].astype(jnp.float32)
    copies[4].wait()
    out_ref[:, 0, 2 * width :] = jnp.broadcast_to(taps[...], key.shape)


def lead_body(parity_ref, own_ref, bank_far, bank_ref, arrived):
    spans = ((0, 0, AHEAD), (AHEAD + 2 * parity_ref[0], AHEAD, 2), (BACK, AHEAD + 2, 3))
    pairs = [(bank_far.at[pl.ds(first, count)], bank_ref.at[pl.ds(place, count)]) for first, place, count in spans]
    for copy in fetch(pairs, arrived):
        copy.wait()


def middle_body(scale, parity_ref, own_ref, other_ref, bank_ref, out_ref):
    parity = parity_ref[0]
    width = bank_ref.shape[2]
    half = width // 2
    rows = 2 * own_ref.shape[0]
    ahead = bank_ref[AHEAD : AHEAD + 2].reshape(2 * width, width)
    signal = jnp.concatenate([own_ref[:, 0, :], other_ref[:, 0, :]], axis=0)
    data = jnp.concatenate(split(signal), axis=0)
    fronts = []
    for index in range(3):
        wide = product(ahead, data[:, index * width : (index + 1) * width])
        fronts.append(wide[: 2 * rows] + wide[2 * rows :])
    twist = [bank_ref[AHEAD + 3 + i].astype(jnp.float32) for i in (0, 1)]
    cosine, sine = [table[:rows] + table[rows:] for table in twist]
    reals = [[] for _ in range(3)]
    imags = [[] for _ in range(3)]
    size = rows // PARTS
    stacks, spectras, mixes, outs = {}, {}, {}, {}
    pieces = [(part, bins) for bins in (0, 1) for part in range(PARTS)]

    def twisted(part):
        here = slice(part * size, (part + 1) * size)
        there = slice(rows + part * size, rows + (part + 1) * size)
        even, odd = [], []
        for index in range(3):
            real = fronts[index][here]
            imag = fronts[index][there]
            real, imag = real * cosine[here] + imag * sine[here], imag * cosine[here] - real * sine[here]
            even.append(jnp.concatenate([real[:, :half] + real[:, half:], imag[:, :half] + imag[:, half:]], axis=1))
            odd.append(jnp.concatenate([real[:, :half] - real[:, half:], imag[:, :half] - imag[:, half:]], axis=1))
        stacks[part, 0] = jnp.concatenate(even, axis=0)
        stacks[part, 1] = jnp.concatenate(odd, axis=0)

    def mix(key):
        spectra = spectras[key]
        gated_real, gated_imag = spectra[:size, :half], spectra[:size, half:]
        grad_real, grad_imag = spectra[size : 2 * size, :half], spectra[size : 2 * size, half:]
        taps_real, taps_imag = spectra[2 * size :, :half], spectra[2 * size :, half:]
        conv_real = gated_real * taps_real - gated_imag * taps_imag
        conv_imag = gated_real * taps_imag + gated_imag * taps_real
        back_real = grad_real * taps_real + grad_imag * taps_imag
        back_imag = grad_imag * taps_real - grad_real * taps_imag
        cross_real = (grad_real * gated_real + grad_imag * gated_imag) * scale
        cross_imag = (grad_imag * gated_real - grad_real * gated_imag) * scale
        mixes[key] = jnp.concatenate(
            [
                jnp.concatenate([conv_real, conv_imag], axis=1),
                jnp.concatenate([back_real, back_imag], axis=1),
                jnp.concatenate([cross_real, cross_imag], axis=1),
            ],
            axis=0,
        )

    def untwist(part):
        here = slice(part * size, (part + 1) * size)
        for index in range(3):
            first = outs[part, 0][index * size : (index + 1) * size]
            second = outs[part, 1][index * size : (index + 1) * size]
            total, difference = first + second, first - second
            real = jnp.concatenate([total[:, :half], difference[:, :half]], axis=1)
            imag = jnp.concatenate([total[:, half:], difference[:, half:]], axis=1)
            reals[index].append(real * cosine[here] - imag * sine[here])
            imags[index].append(real * sine[here] + imag * cosine[here])

    for part in range(PARTS):
        twisted(part)
    for key in pieces:
        spectras[key] = inner_product(stacks[key], bank_ref, key[1], False)
    for key in pieces:
        mix(key)
    for key in pieces:
        outs[key] = inner_product(mixes[key], bank_ref, key[1], True)
    for part in range(PARTS):
        untwist(part)
    table = bank_ref[AHEAD + 2, pl.ds(pl.multiple_of(rows * parity, rows), rows)]
    for index in range(3):
        high, low = split(jnp.concatenate(reals[index] + imags[index], axis=0))
        wide = product(table, high)
        out_ref[:, 0, index * width : (index + 1) * width] = (
            wide[: rows // 2] + wide[rows // 2 :] + product(table[: rows // 2], low)
        )


def sum_body(moved_ref, out_ref):
    width = out_ref.shape[1]
    out_ref[...] = jnp.sum(moved_ref[:, 0, 2 * width :], axis=0, keepdims=True)


def finish_body(moved_ref, key_ref, value_ref, grad_ref, query_out, key_out, value_out):
    width = key_ref.shape[1]
    back = moved_ref[:, 0, width : 2 * width]
    query_out[...] = (grad_ref[...].astype(jnp.float32) * moved_ref[:, 0, :width]).astype(jnp.bfloat16)
    key_out[...] = (back * value_ref[...].astype(jnp.float32)).astype(jnp.bfloat16)
    value_out[...] = (back * key_ref[...].astype(jnp.float32)).astype(jnp.bfloat16)


def add_body(left_ref, right_ref, out_ref):
    out_ref[...] = left_ref[...] + right_ref[...]


def kernel_call(body, out_shape, limit, operands, in_specs, scratch=()):
    return pl.pallas_call(
        body,
        out_shape=out_shape,
        in_specs=in_specs,
        scratch_shapes=scratch,
        compiler_params=pltpu.CompilerParams(vmem_limit_bytes=limit * MIB),
    )(*operands)


def shards(query_proj, key_proj, value_proj, filter_taps, out_grad):
    devices = lax.axis_size("ctx")
    channels, width = query_proj.shape
    chips = devices // 2
    parity = (lax.axis_index("ctx") % 2).astype(jnp.int32).reshape(1)
    same_core = [[int(2 * chip + core) for chip in ORDER] for core in (0, 1)]
    other_core = [(device, device ^ 1) for device in range(devices)]
    scale = 1.0 / math.sqrt(channels * lax.axis_size("ch") * devices * width)
    message = jax.ShapeDtypeStruct((chips, 1, 3 * width), jnp.float32)
    narrow = jax.ShapeDtypeStruct((channels, width), jnp.bfloat16)
    bank = jnp.asarray(table_bank(devices, width))

    def exchange(array):
        return lax.all_to_all(array, "ctx", 0, 0, axis_index_groups=same_core, tiled=True)

    def middle(*refs):
        middle_body(scale, *refs)

    far = pl.BlockSpec(memory_space=pltpu.HBM)
    key_far, value_far, grad_far, query_far, taps_far = [
        pltpu.with_memory_space_constraint(array, pltpu.HBM)
        for array in (key_proj, value_proj, out_grad, query_proj, filter_taps.reshape(1, width))
    ]
    near = pl.BlockSpec(memory_space=pltpu.VMEM)
    scalar = pl.BlockSpec(memory_space=pltpu.SMEM)
    local = pltpu.VMEM((channels, width), jnp.bfloat16)
    packed, key, value, grad = kernel_call(
        pack_body,
        (message, narrow, narrow, narrow),
        4,
        (key_far, value_far, grad_far, query_far, taps_far),
        [far] * 5,
        [local, pltpu.VMEM((1, width), jnp.float32), pltpu.SemaphoreType.DMA((5,))],
    )
    own = exchange(packed)
    other = lax.ppermute(own, "ctx", other_core)
    near_bank = kernel_call(
        lead_body,
        jax.ShapeDtypeStruct((bank.shape[0] - 2,) + bank.shape[1:], bank.dtype),
        8,
        (parity, own, pltpu.with_memory_space_constraint(bank, pltpu.HBM)),
        [scalar, near, far],
        [pltpu.SemaphoreType.DMA((3,))],
    )
    restored = kernel_call(middle, message, 24, (parity, own, other, near_bank), [scalar, near, near, near])
    moved = exchange(restored)
    line = jax.ShapeDtypeStruct((1, width), jnp.float32)
    partial = kernel_call(sum_body, line, 4, (moved,), [near])
    swapped = lax.ppermute(partial, "ch", [(0, 1), (1, 0)])
    query_grad, key_grad, value_grad = kernel_call(
        finish_body, (narrow, narrow, narrow), 4, (moved, key, value, grad), [near] * 4
    )
    filter_grad = kernel_call(add_body, line, 4, (partial, swapped), [near, near]).reshape(width)
    return (query_grad, key_grad, value_grad, filter_grad)


def solution(mesh):
    placed = (P("ch", "ctx"), P("ch", "ctx"), P("ch", "ctx"), P("ctx"), P("ch", "ctx"))
    return jax.shard_map(
        shards,
        mesh=mesh,
        in_specs=placed,
        out_specs=(P("ch", "ctx"), P("ch", "ctx"), P("ch", "ctx"), P("ctx")),
        check_vma=False,
    )
```

```python
import math

import jax
import jax.numpy as jnp
import numpy as np
from jax import lax
from jax.experimental import pallas as pl
from jax.experimental.pallas import tpu as pltpu
from jax.sharding import PartitionSpec as P

SHIFT = 0.25
MIB = 1024 * 1024
PARTS = 2
ORDER = np.array([((1 - x) * 8 + (4 + 3 * z) % 8) * 4 + (2 + y) % 4 for z in range(8) for y in range(4) for x in range(2)])
AHEAD, BACK, TWIST = 4, 6, 7


def halves(values):
    high = values.astype(jnp.bfloat16)
    low = (values - np.asarray(high).astype(np.float64)).astype(jnp.bfloat16)
    return np.asarray(high), np.asarray(low)


def table_bank(blocks, width):
    length = blocks * width
    half = width // 2
    rows = np.arange(blocks) + SHIFT
    planes = []
    for odd in (0, 1):
        angle = 2.0 * math.pi * (np.outer(np.arange(half), 2 * np.arange(half) + odd) % width) / width
        cosine, sine = np.cos(angle), np.sin(angle)
        planes += halves(np.block([[cosine, -sine], [sine, cosine]]))
    block_angle = 2.0 * math.pi * np.outer(rows, np.arange(blocks)) / blocks
    block_table = np.concatenate([np.cos(block_angle), -np.sin(block_angle)], axis=0)
    own = [2 * ORDER + parity for parity in (0, 1)]
    for e in (0, 1):
        planes.append(np.concatenate(halves(block_table[:, own[e]]) * 2, axis=1))
    pieces = [np.concatenate(halves(block_table.T[own[e]] / length), axis=0) for e in (0, 1)]
    planes.append(np.concatenate(pieces, axis=0))
    twist_angle = 2.0 * math.pi * np.outer(rows, np.arange(width)) / length
    planes += [np.concatenate(halves(np.cos(twist_angle)), axis=0), np.concatenate(halves(np.sin(twist_angle)), axis=0)]
    return np.stack(planes)


def split(values):
    high = values.astype(jnp.bfloat16)
    return high, (values - high.astype(jnp.float32)).astype(jnp.bfloat16)


def product(left, right, transposed=False):
    contracted = (((1,), (1 if transposed else 0,)), ((), ()))
    return lax.dot_general(left, right, contracted, preferred_element_type=jnp.float32)


def inner_product(values, bank_ref, odd, transposed):
    count = values.shape[0]
    high, low = split(values)
    wide = product(jnp.concatenate([high, low], axis=0), bank_ref[2 * odd], transposed)
    return wide[:count] + wide[count:] + product(high, bank_ref[2 * odd + 1], transposed)


def fetch(pairs, arrived):
    copies = [pltpu.make_async_copy(source, here, arrived.at[i]) for i, (source, here) in enumerate(pairs)]
    for copy in copies:
        copy.start()
    return copies


def pack_body(key_far, value_far, grad_far, query_far, taps_far, out_ref, key, value, grad, query, taps, arrived):
    width = key.shape[1]
    copies = fetch(
        ((key_far, key), (value_far, value), (grad_far, grad), (query_far, query), (taps_far, taps)), arrived
    )
    copies[0].wait()
    copies[1].wait()
    out_ref[:, 0, :width] = key[...].astype(jnp.float32) * value[...].astype(jnp.float32)
    copies[2].wait()
    copies[3].wait()
    out_ref[:, 0, width : 2 * width] = grad[...].astype(jnp.float32) * query[...].astype(jnp.float32)
    copies[4].wait()
    out_ref[:, 0, 2 * width :] = jnp.broadcast_to(taps[...], key.shape)


def front_products(blocks_ref, table):
    width = table.shape[1]
    twice = jnp.concatenate([blocks_ref[:, 0, :], blocks_ref[:, 0, :]], axis=0)
    data = jnp.concatenate(split(twice), axis=0)
    return [product(table, data[:, index * width : (index + 1) * width]) for index in range(3)]


def lead_body(parity_ref, own_ref, bank_far, bank_ref, front_ref, arrived):
    spans = ((AHEAD, 2), (0, AHEAD), (BACK, 3))
    pairs = [(bank_far.at[pl.ds(first, count)], bank_ref.at[pl.ds(first, count)]) for first, count in spans]
    copies = fetch(pairs, arrived)
    copies[0].wait()
    for index, front in enumerate(front_products(own_ref, bank_ref[AHEAD + parity_ref[0]])):
        front_ref[index] = front
    copies[1].wait()
    copies[2].wait()


def middle_body(scale, parity_ref, other_ref, front_ref, bank_ref, out_ref):
    parity = parity_ref[0]
    width = bank_ref.shape[2]
    half = width // 2
    rows = 2 * other_ref.shape[0]
    others = front_products(other_ref, bank_ref[AHEAD + 1 - parity])
    fronts = [front_ref[index] + others[index] for index in range(3)]
    twist = [bank_ref[TWIST + i].astype(jnp.float32) for i in (0, 1)]
    cosine, sine = [table[:rows] + table[rows:] for table in twist]
    reals = [[] for _ in range(3)]
    imags = [[] for _ in range(3)]
    size = rows // PARTS
    stacks, spectras, mixes, outs = {}, {}, {}, {}
    pieces = [(part, bins) for bins in (0, 1) for part in range(PARTS)]

    def twisted(part):
        here = slice(part * size, (part + 1) * size)
        there = slice(rows + part * size, rows + (part + 1) * size)
        even, odd = [], []
        for index in range(3):
            real = fronts[index][here]
            imag = fronts[index][there]
            real, imag = real * cosine[here] + imag * sine[here], imag * cosine[here] - real * sine[here]
            even.append(jnp.concatenate([real[:, :half] + real[:, half:], imag[:, :half] + imag[:, half:]], axis=1))
            odd.append(jnp.concatenate([real[:, :half] - real[:, half:], imag[:, :half] - imag[:, half:]], axis=1))
        stacks[part, 0] = jnp.concatenate(even, axis=0)
        stacks[part, 1] = jnp.concatenate(odd, axis=0)

    def mix(key):
        spectra = spectras[key]
        gated_real, gated_imag = spectra[:size, :half], spectra[:size, half:]
        grad_real, grad_imag = spectra[size : 2 * size, :half], spectra[size : 2 * size, half:]
        taps_real, taps_imag = spectra[2 * size :, :half], spectra[2 * size :, half:]
        conv_real = gated_real * taps_real - gated_imag * taps_imag
        conv_imag = gated_real * taps_imag + gated_imag * taps_real
        back_real = grad_real * taps_real + grad_imag * taps_imag
        back_imag = grad_imag * taps_real - grad_real * taps_imag
        cross_real = (grad_real * gated_real + grad_imag * gated_imag) * scale
        cross_imag = (grad_imag * gated_real - grad_real * gated_imag) * scale
        mixes[key] = jnp.concatenate(
            [
                jnp.concatenate([conv_real, conv_imag], axis=1),
                jnp.concatenate([back_real, back_imag], axis=1),
                jnp.concatenate([cross_real, cross_imag], axis=1),
            ],
            axis=0,
        )

    def untwist(part):
        here = slice(part * size, (part + 1) * size)
        for index in range(3):
            first = outs[part, 0][index * size : (index + 1) * size]
            second = outs[part, 1][index * size : (index + 1) * size]
            total, difference = first + second, first - second
            real = jnp.concatenate([total[:, :half], difference[:, :half]], axis=1)
            imag = jnp.concatenate([total[:, half:], difference[:, half:]], axis=1)
            reals[index].append(real * cosine[here] - imag * sine[here])
            imags[index].append(real * sine[here] + imag * cosine[here])

    for part in range(PARTS):
        twisted(part)
    for key in pieces:
        spectras[key] = inner_product(stacks[key], bank_ref, key[1], False)
    for key in pieces:
        mix(key)
    for key in pieces:
        outs[key] = inner_product(mixes[key], bank_ref, key[1], True)
    for part in range(PARTS):
        untwist(part)
    table = bank_ref[BACK, pl.ds(pl.multiple_of(rows * parity, rows), rows)]
    for index in range(3):
        high, low = split(jnp.concatenate(reals[index] + imags[index], axis=0))
        wide = product(table, high)
        out_ref[:, 0, index * width : (index + 1) * width] = (
            wide[: rows // 2] + wide[rows // 2 :] + product(table[: rows // 2], low)
        )


def sum_body(moved_ref, out_ref):
    width = out_ref.shape[1]
    out_ref[...] = jnp.sum(moved_ref[:, 0, 2 * width :], axis=0, keepdims=True)


def finish_body(moved_ref, key_ref, value_ref, grad_ref, query_out, key_out, value_out):
    width = key_ref.shape[1]
    back = moved_ref[:, 0, width : 2 * width]
    query_out[...] = (grad_ref[...].astype(jnp.float32) * moved_ref[:, 0, :width]).astype(jnp.bfloat16)
    key_out[...] = (back * value_ref[...].astype(jnp.float32)).astype(jnp.bfloat16)
    value_out[...] = (back * key_ref[...].astype(jnp.float32)).astype(jnp.bfloat16)


def add_body(left_ref, right_ref, out_ref):
    out_ref[...] = left_ref[...] + right_ref[...]


def kernel_call(body, out_shape, limit, operands, in_specs, scratch=()):
    return pl.pallas_call(
        body,
        out_shape=out_shape,
        in_specs=in_specs,
        scratch_shapes=scratch,
        compiler_params=pltpu.CompilerParams(vmem_limit_bytes=limit * MIB),
    )(*operands)


def shards(query_proj, key_proj, value_proj, filter_taps, out_grad):
    devices = lax.axis_size("ctx")
    channels, width = query_proj.shape
    chips = devices // 2
    parity = (lax.axis_index("ctx") % 2).astype(jnp.int32).reshape(1)
    same_core = [[int(2 * chip + core) for chip in ORDER] for core in (0, 1)]
    other_core = [(device, device ^ 1) for device in range(devices)]
    scale = 1.0 / math.sqrt(channels * lax.axis_size("ch") * devices * width)
    message = jax.ShapeDtypeStruct((chips, 1, 3 * width), jnp.float32)
    narrow = jax.ShapeDtypeStruct((channels, width), jnp.bfloat16)
    bank = jnp.asarray(table_bank(devices, width))

    def exchange(array):
        return lax.all_to_all(array, "ctx", 0, 0, axis_index_groups=same_core, tiled=True)

    def middle(*refs):
        middle_body(scale, *refs)

    far = pl.BlockSpec(memory_space=pltpu.HBM)
    key_far, value_far, grad_far, query_far, taps_far = [
        pltpu.with_memory_space_constraint(array, pltpu.HBM)
        for array in (key_proj, value_proj, out_grad, query_proj, filter_taps.reshape(1, width))
    ]
    near = pl.BlockSpec(memory_space=pltpu.VMEM)
    scalar = pl.BlockSpec(memory_space=pltpu.SMEM)
    local = pltpu.VMEM((channels, width), jnp.bfloat16)
    packed, key, value, grad = kernel_call(
        pack_body,
        (message, narrow, narrow, narrow),
        4,
        (key_far, value_far, grad_far, query_far, taps_far),
        [far] * 5,
        [local, pltpu.VMEM((1, width), jnp.float32), pltpu.SemaphoreType.DMA((5,))],
    )
    own = exchange(packed)
    other = lax.ppermute(own, "ctx", other_core)
    near_bank, front = kernel_call(
        lead_body,
        (
            jax.ShapeDtypeStruct(bank.shape, bank.dtype),
            jax.ShapeDtypeStruct((3, 2 * devices, width), jnp.float32),
        ),
        8,
        (parity, own, pltpu.with_memory_space_constraint(bank, pltpu.HBM)),
        [scalar, near, far],
        [pltpu.SemaphoreType.DMA((3,))],
    )
    restored = kernel_call(middle, message, 24, (parity, other, front, near_bank), [scalar, near, near, near])
    moved = exchange(restored)
    line = jax.ShapeDtypeStruct((1, width), jnp.float32)
    partial = kernel_call(sum_body, line, 4, (moved,), [near])
    swapped = lax.ppermute(partial, "ch", [(0, 1), (1, 0)])
    query_grad, key_grad, value_grad = kernel_call(
        finish_body, (narrow, narrow, narrow), 4, (moved, key, value, grad), [near] * 4
    )
    filter_grad = kernel_call(add_body, line, 4, (partial, swapped), [near, near]).reshape(width)
    return (query_grad, key_grad, value_grad, filter_grad)


def solution(mesh):
    placed = (P("ch", "ctx"), P("ch", "ctx"), P("ch", "ctx"), P("ctx"), P("ch", "ctx"))
    return jax.shard_map(
        shards,
        mesh=mesh,
        in_specs=placed,
        out_specs=(P("ch", "ctx"), P("ch", "ctx"), P("ch", "ctx"), P("ctx")),
        check_vma=False,
    )
```

```python
import math

import jax
import jax.numpy as jnp
import numpy as np
from jax import lax
from jax.experimental import pallas as pl
from jax.experimental.pallas import tpu as pltpu
from jax.sharding import PartitionSpec as P

SHIFT = 0.25
MIB = 1024 * 1024
PARTS = 2
ORDER = np.array([((1 - x) * 8 + (4 + 3 * z) % 8) * 4 + (2 + y) % 4 for z in range(8) for y in range(4) for x in range(2)])
AHEAD, BACK, TWIST = 4, 6, 7


def halves(values):
    high = values.astype(jnp.bfloat16)
    low = (values - np.asarray(high).astype(np.float64)).astype(jnp.bfloat16)
    return np.asarray(high), np.asarray(low)


def table_bank(blocks, width):
    length = blocks * width
    half = width // 2
    rows = np.arange(blocks) + SHIFT
    planes = []
    for odd in (0, 1):
        angle = 2.0 * math.pi * (np.outer(np.arange(half), 2 * np.arange(half) + odd) % width) / width
        cosine, sine = np.cos(angle), np.sin(angle)
        planes += halves(np.block([[cosine, -sine], [sine, cosine]]))
    block_angle = 2.0 * math.pi * np.outer(rows, np.arange(blocks)) / blocks
    block_table = np.concatenate([np.cos(block_angle), -np.sin(block_angle)], axis=0)
    own = [2 * ORDER + parity for parity in (0, 1)]
    for e in (0, 1):
        planes.append(np.concatenate(halves(block_table[:, own[e]]) * 2, axis=1))
    pieces = [np.concatenate(halves(block_table.T[own[e]] / length), axis=0) for e in (0, 1)]
    planes.append(np.concatenate(pieces, axis=0))
    twist_angle = 2.0 * math.pi * np.outer(rows, np.arange(width)) / length
    planes += [np.concatenate(halves(np.cos(twist_angle)), axis=0), np.concatenate(halves(np.sin(twist_angle)), axis=0)]
    return np.stack(planes)


def split(values):
    high = values.astype(jnp.bfloat16)
    return high, (values - high.astype(jnp.float32)).astype(jnp.bfloat16)


def product(left, right, transposed=False):
    contracted = (((1,), (1 if transposed else 0,)), ((), ()))
    return lax.dot_general(left, right, contracted, preferred_element_type=jnp.float32)


def inner_product(values, bank_ref, odd, transposed):
    count = values.shape[0]
    high, low = split(values)
    wide = product(jnp.concatenate([high, low], axis=0), bank_ref[2 * odd], transposed)
    return wide[:count] + wide[count:] + product(high, bank_ref[2 * odd + 1], transposed)


def fetch(pairs, arrived):
    copies = [pltpu.make_async_copy(source, here, arrived.at[i]) for i, (source, here) in enumerate(pairs)]
    for copy in copies:
        copy.start()
    return copies


def pack_body(key_far, value_far, grad_far, query_far, taps_far, out_ref, key, value, grad, query, taps, arrived):
    width = key.shape[1]
    copies = fetch(
        ((key_far, key), (value_far, value), (grad_far, grad), (query_far, query), (taps_far, taps)), arrived
    )
    copies[0].wait()
    copies[1].wait()
    out_ref[:, 0, :width] = key[...].astype(jnp.float32) * value[...].astype(jnp.float32)
    copies[2].wait()
    copies[3].wait()
    out_ref[:, 0, width : 2 * width] = grad[...].astype(jnp.float32) * query[...].astype(jnp.float32)
    copies[4].wait()
    out_ref[:, 0, 2 * width :] = jnp.broadcast_to(taps[...], key.shape)


def front_products(blocks_ref, table):
    width = table.shape[1]
    twice = jnp.concatenate([blocks_ref[:, 0, :], blocks_ref[:, 0, :]], axis=0)
    data = jnp.concatenate(split(twice), axis=0)
    return [product(table, data[:, index * width : (index + 1) * width]) for index in range(3)]


def lead_body(parity_ref, own_ref, bank_far, bank_ref, front_ref, arrived):
    spans = ((AHEAD, 2), (0, AHEAD), (BACK, 3))
    pairs = [(bank_far.at[pl.ds(first, count)], bank_ref.at[pl.ds(first, count)]) for first, count in spans]
    copies = fetch(pairs, arrived)
    copies[0].wait()
    for index, front in enumerate(front_products(own_ref, bank_ref[AHEAD + parity_ref[0]])):
        front_ref[index] = front
    copies[1].wait()
    copies[2].wait()


def middle_body(scale, parity_ref, other_ref, front_ref, bank_ref, out_ref):
    parity = parity_ref[0]
    width = bank_ref.shape[2]
    half = width // 2
    rows = 2 * other_ref.shape[0]
    others = front_products(other_ref, bank_ref[AHEAD + 1 - parity])
    fronts = [front_ref[index] + others[index] for index in range(3)]
    twist = [bank_ref[TWIST + i].astype(jnp.float32) for i in (0, 1)]
    cosine, sine = [table[:rows] + table[rows:] for table in twist]
    reals = [[] for _ in range(3)]
    imags = [[] for _ in range(3)]
    size = rows // PARTS
    stacks, spectras, mixes, outs = {}, {}, {}, {}
    pieces = [(part, bins) for bins in (0, 1) for part in range(PARTS)]

    def twisted(part):
        here = slice(part * size, (part + 1) * size)
        there = slice(rows + part * size, rows + (part + 1) * size)
        even, odd = [], []
        for index in range(3):
            real = fronts[index][here]
            imag = fronts[index][there]
            real, imag = real * cosine[here] + imag * sine[here], imag * cosine[here] - real * sine[here]
            even.append(jnp.concatenate([real[:, :half] + real[:, half:], imag[:, :half] + imag[:, half:]], axis=1))
            odd.append(jnp.concatenate([real[:, :half] - real[:, half:], imag[:, :half] - imag[:, half:]], axis=1))
        stacks[part, 0] = jnp.concatenate(even, axis=0)
        stacks[part, 1] = jnp.concatenate(odd, axis=0)

    def mix(key):
        spectra = spectras[key]
        gated_real, gated_imag = spectra[:size, :half], spectra[:size, half:]
        grad_real, grad_imag = spectra[size : 2 * size, :half], spectra[size : 2 * size, half:]
        taps_real, taps_imag = spectra[2 * size :, :half], spectra[2 * size :, half:]
        conv_real = gated_real * taps_real - gated_imag * taps_imag
        conv_imag = gated_real * taps_imag + gated_imag * taps_real
        back_real = grad_real * taps_real + grad_imag * taps_imag
        back_imag = grad_imag * taps_real - grad_real * taps_imag
        cross_real = (grad_real * gated_real + grad_imag * gated_imag) * scale
        cross_imag = (grad_imag * gated_real - grad_real * gated_imag) * scale
        mixes[key] = jnp.concatenate(
            [
                jnp.concatenate([conv_real, conv_imag], axis=1),
                jnp.concatenate([back_real, back_imag], axis=1),
                jnp.concatenate([cross_real, cross_imag], axis=1),
            ],
            axis=0,
        )

    def untwist(part):
        here = slice(part * size, (part + 1) * size)
        for index in range(3):
            first = outs[part, 0][index * size : (index + 1) * size]
            second = outs[part, 1][index * size : (index + 1) * size]
            total, difference = first + second, first - second
            real = jnp.concatenate([total[:, :half], difference[:, :half]], axis=1)
            imag = jnp.concatenate([total[:, half:], difference[:, half:]], axis=1)
            reals[index].append(real * cosine[here] - imag * sine[here])
            imags[index].append(real * sine[here] + imag * cosine[here])

    for part in range(PARTS):
        twisted(part)
    for key in pieces:
        spectras[key] = inner_product(stacks[key], bank_ref, key[1], False)
    for key in pieces:
        mix(key)
    for key in pieces:
        outs[key] = inner_product(mixes[key], bank_ref, key[1], True)
    for part in range(PARTS):
        untwist(part)
    table = bank_ref[BACK, pl.ds(pl.multiple_of(rows * parity, rows), rows)]
    for index in range(3):
        high, low = split(jnp.concatenate(reals[index] + imags[index], axis=0))
        wide = product(table, high)
        out_ref[:, 0, index * width : (index + 1) * width] = (
            wide[: rows // 2] + wide[rows // 2 :] + product(table[: rows // 2], low)
        )


def sum_body(moved_ref, out_ref):
    width = out_ref.shape[1]
    out_ref[...] = jnp.sum(moved_ref[:, 0, 2 * width :], axis=0, keepdims=True)


def finish_body(moved_ref, key_ref, value_ref, grad_ref, left_ref, right_ref, query_out, key_out, value_out, filter_out):
    width = key_ref.shape[1]
    filter_out[...] = left_ref[...] + right_ref[...]
    back = moved_ref[:, 0, width : 2 * width]
    query_out[...] = (grad_ref[...].astype(jnp.float32) * moved_ref[:, 0, :width]).astype(jnp.bfloat16)
    key_out[...] = (back * value_ref[...].astype(jnp.float32)).astype(jnp.bfloat16)
    value_out[...] = (back * key_ref[...].astype(jnp.float32)).astype(jnp.bfloat16)


def kernel_call(body, out_shape, limit, operands, in_specs, scratch=()):
    return pl.pallas_call(
        body,
        out_shape=out_shape,
        in_specs=in_specs,
        scratch_shapes=scratch,
        compiler_params=pltpu.CompilerParams(vmem_limit_bytes=limit * MIB),
    )(*operands)


def shards(query_proj, key_proj, value_proj, filter_taps, out_grad):
    devices = lax.axis_size("ctx")
    channels, width = query_proj.shape
    chips = devices // 2
    parity = (lax.axis_index("ctx") % 2).astype(jnp.int32).reshape(1)
    same_core = [[int(2 * chip + core) for chip in ORDER] for core in (0, 1)]
    other_core = [(device, device ^ 1) for device in range(devices)]
    scale = 1.0 / math.sqrt(channels * lax.axis_size("ch") * devices * width)
    message = jax.ShapeDtypeStruct((chips, 1, 3 * width), jnp.float32)
    narrow = jax.ShapeDtypeStruct((channels, width), jnp.bfloat16)
    bank = jnp.asarray(table_bank(devices, width))

    def exchange(array):
        return lax.all_to_all(array, "ctx", 0, 0, axis_index_groups=same_core, tiled=True)

    def middle(*refs):
        middle_body(scale, *refs)

    far = pl.BlockSpec(memory_space=pltpu.HBM)
    key_far, value_far, grad_far, query_far, taps_far = [
        pltpu.with_memory_space_constraint(array, pltpu.HBM)
        for array in (key_proj, value_proj, out_grad, query_proj, filter_taps.reshape(1, width))
    ]
    near = pl.BlockSpec(memory_space=pltpu.VMEM)
    scalar = pl.BlockSpec(memory_space=pltpu.SMEM)
    local = pltpu.VMEM((channels, width), jnp.bfloat16)
    packed, key, value, grad = kernel_call(
        pack_body,
        (message, narrow, narrow, narrow),
        4,
        (key_far, value_far, grad_far, query_far, taps_far),
        [far] * 5,
        [local, pltpu.VMEM((1, width), jnp.float32), pltpu.SemaphoreType.DMA((5,))],
    )
    own = exchange(packed)
    other = lax.ppermute(own, "ctx", other_core)
    near_bank, front = kernel_call(
        lead_body,
        (
            jax.ShapeDtypeStruct(bank.shape, bank.dtype),
            jax.ShapeDtypeStruct((3, 2 * devices, width), jnp.float32),
        ),
        8,
        (parity, own, pltpu.with_memory_space_constraint(bank, pltpu.HBM)),
        [scalar, near, far],
        [pltpu.SemaphoreType.DMA((3,))],
    )
    restored = kernel_call(middle, message, 24, (parity, other, front, near_bank), [scalar, near, near, near])
    moved = exchange(restored)
    line = jax.ShapeDtypeStruct((1, width), jnp.float32)
    partial = kernel_call(sum_body, line, 4, (moved,), [near])
    swapped = lax.ppermute(partial, "ch", [(0, 1), (1, 0)])
    query_grad, key_grad, value_grad, filter_grad = kernel_call(
        finish_body, (narrow, narrow, narrow, line), 4, (moved, key, value, grad, partial, swapped), [near] * 6
    )
    filter_grad = filter_grad.reshape(width)
    return (query_grad, key_grad, value_grad, filter_grad)


def solution(mesh):
    placed = (P("ch", "ctx"), P("ch", "ctx"), P("ch", "ctx"), P("ctx"), P("ch", "ctx"))
    return jax.shard_map(
        shards,
        mesh=mesh,
        in_specs=placed,
        out_specs=(P("ch", "ctx"), P("ch", "ctx"), P("ch", "ctx"), P("ctx")),
        check_vma=False,
    )
```

```python
import math

import jax
import jax.numpy as jnp
import numpy as np
from jax import lax
from jax.experimental import pallas as pl
from jax.experimental.pallas import tpu as pltpu
from jax.sharding import PartitionSpec as P

SHIFT = 0.25
MIB = 1024 * 1024
PARTS = 2
ORDER = np.array([((1 - x) * 8 + (4 + 3 * z) % 8) * 4 + (2 + y) % 4 for z in range(8) for y in range(4) for x in range(2)])
AHEAD, BACK, TWIST = 4, 6, 7


def halves(values):
    high = values.astype(jnp.bfloat16)
    low = (values - np.asarray(high).astype(np.float64)).astype(jnp.bfloat16)
    return np.asarray(high), np.asarray(low)


def table_bank(blocks, width):
    length = blocks * width
    half = width // 2
    rows = np.arange(blocks) + SHIFT
    planes = []
    for odd in (0, 1):
        angle = 2.0 * math.pi * (np.outer(np.arange(half), 2 * np.arange(half) + odd) % width) / width
        cosine, sine = np.cos(angle), np.sin(angle)
        planes += halves(np.block([[cosine, -sine], [sine, cosine]]))
    block_angle = 2.0 * math.pi * np.outer(rows, np.arange(blocks)) / blocks
    block_table = np.concatenate([np.cos(block_angle), -np.sin(block_angle)], axis=0)
    own = [2 * ORDER + parity for parity in (0, 1)]
    for e in (0, 1):
        planes.append(np.concatenate(halves(block_table[:, own[e]]) * 2, axis=1))
    pieces = [np.concatenate(halves(block_table.T[own[e]] / length), axis=0) for e in (0, 1)]
    planes.append(np.concatenate(pieces, axis=0))
    twist_angle = 2.0 * math.pi * np.outer(rows, np.arange(width)) / length
    planes += [np.concatenate(halves(np.cos(twist_angle)), axis=0), np.concatenate(halves(np.sin(twist_angle)), axis=0)]
    return np.stack(planes)


def split(values):
    high = values.astype(jnp.bfloat16)
    return high, (values - high.astype(jnp.float32)).astype(jnp.bfloat16)


def product(left, right, transposed=False):
    contracted = (((1,), (1 if transposed else 0,)), ((), ()))
    return lax.dot_general(left, right, contracted, preferred_element_type=jnp.float32)


def inner_product(values, bank_ref, odd, transposed):
    count = values.shape[0]
    high, low = split(values)
    wide = product(jnp.concatenate([high, low], axis=0), bank_ref[2 * odd], transposed)
    return wide[:count] + wide[count:] + product(high, bank_ref[2 * odd + 1], transposed)


def fetch(pairs, arrived):
    copies = [pltpu.make_async_copy(source, here, arrived.at[i]) for i, (source, here) in enumerate(pairs)]
    for copy in copies:
        copy.start()
    return copies


def pack_body(key_far, value_far, grad_far, query_far, taps_far, out_ref, key, value, grad, query, taps, arrived):
    width = key.shape[1]
    copies = fetch(
        ((key_far, key), (value_far, value), (grad_far, grad), (query_far, query), (taps_far, taps)), arrived
    )
    copies[0].wait()
    copies[1].wait()
    out_ref[:, 0, :width] = key[...].astype(jnp.float32) * value[...].astype(jnp.float32)
    copies[2].wait()
    copies[3].wait()
    out_ref[:, 0, width : 2 * width] = grad[...].astype(jnp.float32) * query[...].astype(jnp.float32)
    copies[4].wait()
    out_ref[:, 0, 2 * width :] = jnp.broadcast_to(taps[...], key.shape)


def front_products(blocks_ref, table):
    width = table.shape[1]
    twice = jnp.concatenate([blocks_ref[:, 0, :], blocks_ref[:, 0, :]], axis=0)
    data = jnp.concatenate(split(twice), axis=0)
    return [product(table, data[:, index * width : (index + 1) * width]) for index in range(3)]


def lead_body(parity_ref, own_ref, bank_far, bank_ref, front_ref, twist_ref, arrived):
    spans = ((AHEAD, 2), (0, AHEAD), (BACK, 3))
    pairs = [(bank_far.at[pl.ds(first, count)], bank_ref.at[pl.ds(first, count)]) for first, count in spans]
    copies = fetch(pairs, arrived)
    copies[0].wait()
    for index, front in enumerate(front_products(own_ref, bank_ref[AHEAD + parity_ref[0]])):
        front_ref[index] = front
    copies[2].wait()
    rows = twist_ref.shape[1]
    for index in (0, 1):
        table = bank_ref[TWIST + index].astype(jnp.float32)
        twist_ref[index] = table[:rows] + table[rows:]
    copies[1].wait()


def middle_body(scale, parity_ref, other_ref, front_ref, twist_ref, bank_ref, out_ref):
    parity = parity_ref[0]
    width = bank_ref.shape[2]
    half = width // 2
    rows = 2 * other_ref.shape[0]
    others = front_products(other_ref, bank_ref[AHEAD + 1 - parity])
    fronts = [front_ref[index] + others[index] for index in range(3)]
    cosine, sine = twist_ref[0], twist_ref[1]
    reals = [[] for _ in range(3)]
    imags = [[] for _ in range(3)]
    size = rows // PARTS
    stacks, spectras, mixes, outs = {}, {}, {}, {}
    pieces = [(part, bins) for bins in (0, 1) for part in range(PARTS)]

    def twisted(part):
        here = slice(part * size, (part + 1) * size)
        there = slice(rows + part * size, rows + (part + 1) * size)
        even, odd = [], []
        for index in range(3):
            real = fronts[index][here]
            imag = fronts[index][there]
            real, imag = real * cosine[here] + imag * sine[here], imag * cosine[here] - real * sine[here]
            even.append(jnp.concatenate([real[:, :half] + real[:, half:], imag[:, :half] + imag[:, half:]], axis=1))
            odd.append(jnp.concatenate([real[:, :half] - real[:, half:], imag[:, :half] - imag[:, half:]], axis=1))
        stacks[part, 0] = jnp.concatenate(even, axis=0)
        stacks[part, 1] = jnp.concatenate(odd, axis=0)

    def mix(key):
        spectra = spectras[key]
        gated_real, gated_imag = spectra[:size, :half], spectra[:size, half:]
        grad_real, grad_imag = spectra[size : 2 * size, :half], spectra[size : 2 * size, half:]
        taps_real, taps_imag = spectra[2 * size :, :half], spectra[2 * size :, half:]
        conv_real = gated_real * taps_real - gated_imag * taps_imag
        conv_imag = gated_real * taps_imag + gated_imag * taps_real
        back_real = grad_real * taps_real + grad_imag * taps_imag
        back_imag = grad_imag * taps_real - grad_real * taps_imag
        cross_real = (grad_real * gated_real + grad_imag * gated_imag) * scale
        cross_imag = (grad_imag * gated_real - grad_real * gated_imag) * scale
        mixes[key] = jnp.concatenate(
            [
                jnp.concatenate([conv_real, conv_imag], axis=1),
                jnp.concatenate([back_real, back_imag], axis=1),
                jnp.concatenate([cross_real, cross_imag], axis=1),
            ],
            axis=0,
        )

    def untwist(part):
        here = slice(part * size, (part + 1) * size)
        for index in range(3):
            first = outs[part, 0][index * size : (index + 1) * size]
            second = outs[part, 1][index * size : (index + 1) * size]
            total, difference = first + second, first - second
            real = jnp.concatenate([total[:, :half], difference[:, :half]], axis=1)
            imag = jnp.concatenate([total[:, half:], difference[:, half:]], axis=1)
            reals[index].append(real * cosine[here] - imag * sine[here])
            imags[index].append(real * sine[here] + imag * cosine[here])

    for part in range(PARTS):
        twisted(part)
    for key in pieces:
        spectras[key] = inner_product(stacks[key], bank_ref, key[1], False)
    for key in pieces:
        mix(key)
    for key in pieces:
        outs[key] = inner_product(mixes[key], bank_ref, key[1], True)
    for part in range(PARTS):
        untwist(part)
    table = bank_ref[BACK, pl.ds(pl.multiple_of(rows * parity, rows), rows)]
    for index in range(3):
        high, low = split(jnp.concatenate(reals[index] + imags[index], axis=0))
        wide = product(table, high)
        out_ref[:, 0, index * width : (index + 1) * width] = (
            wide[: rows // 2] + wide[rows // 2 :] + product(table[: rows // 2], low)
        )


def sum_body(moved_ref, out_ref):
    width = out_ref.shape[1]
    out_ref[...] = jnp.sum(moved_ref[:, 0, 2 * width :], axis=0, keepdims=True)


def finish_body(moved_ref, key_ref, value_ref, grad_ref, query_out, key_out, value_out):
    width = key_ref.shape[1]
    back = moved_ref[:, 0, width : 2 * width]
    query_out[...] = (grad_ref[...].astype(jnp.float32) * moved_ref[:, 0, :width]).astype(jnp.bfloat16)
    key_out[...] = (back * value_ref[...].astype(jnp.float32)).astype(jnp.bfloat16)
    value_out[...] = (back * key_ref[...].astype(jnp.float32)).astype(jnp.bfloat16)


def add_body(left_ref, right_ref, out_ref):
    out_ref[...] = left_ref[...] + right_ref[...]


def kernel_call(body, out_shape, limit, operands, in_specs, scratch=()):
    return pl.pallas_call(
        body,
        out_shape=out_shape,
        in_specs=in_specs,
        scratch_shapes=scratch,
        compiler_params=pltpu.CompilerParams(vmem_limit_bytes=limit * MIB),
    )(*operands)


def shards(query_proj, key_proj, value_proj, filter_taps, out_grad):
    devices = lax.axis_size("ctx")
    channels, width = query_proj.shape
    chips = devices // 2
    parity = (lax.axis_index("ctx") % 2).astype(jnp.int32).reshape(1)
    same_core = [[int(2 * chip + core) for chip in ORDER] for core in (0, 1)]
    other_core = [(device, device ^ 1) for device in range(devices)]
    scale = 1.0 / math.sqrt(channels * lax.axis_size("ch") * devices * width)
    message = jax.ShapeDtypeStruct((chips, 1, 3 * width), jnp.float32)
    narrow = jax.ShapeDtypeStruct((channels, width), jnp.bfloat16)
    bank = jnp.asarray(table_bank(devices, width))

    def exchange(array):
        return lax.all_to_all(array, "ctx", 0, 0, axis_index_groups=same_core, tiled=True)

    def middle(*refs):
        middle_body(scale, *refs)

    far = pl.BlockSpec(memory_space=pltpu.HBM)
    key_far, value_far, grad_far, query_far, taps_far = [
        pltpu.with_memory_space_constraint(array, pltpu.HBM)
        for array in (key_proj, value_proj, out_grad, query_proj, filter_taps.reshape(1, width))
    ]
    near = pl.BlockSpec(memory_space=pltpu.VMEM)
    scalar = pl.BlockSpec(memory_space=pltpu.SMEM)
    local = pltpu.VMEM((channels, width), jnp.bfloat16)
    packed, key, value, grad = kernel_call(
        pack_body,
        (message, narrow, narrow, narrow),
        4,
        (key_far, value_far, grad_far, query_far, taps_far),
        [far] * 5,
        [local, pltpu.VMEM((1, width), jnp.float32), pltpu.SemaphoreType.DMA((5,))],
    )
    own = exchange(packed)
    other = lax.ppermute(own, "ctx", other_core)
    near_bank, front, twist = kernel_call(
        lead_body,
        (
            jax.ShapeDtypeStruct(bank.shape, bank.dtype),
            jax.ShapeDtypeStruct((3, 2 * devices, width), jnp.float32),
            jax.ShapeDtypeStruct((2, devices, width), jnp.float32),
        ),
        8,
        (parity, own, pltpu.with_memory_space_constraint(bank, pltpu.HBM)),
        [scalar, near, far],
        [pltpu.SemaphoreType.DMA((3,))],
    )
    restored = kernel_call(middle, message, 24, (parity, other, front, twist, near_bank), [scalar] + [near] * 4)
    moved = exchange(restored)
    line = jax.ShapeDtypeStruct((1, width), jnp.float32)
    partial = kernel_call(sum_body, line, 4, (moved,), [near])
    swapped = lax.ppermute(partial, "ch", [(0, 1), (1, 0)])
    query_grad, key_grad, value_grad = kernel_call(
        finish_body, (narrow, narrow, narrow), 4, (moved, key, value, grad), [near] * 4
    )
    filter_grad = kernel_call(add_body, line, 4, (partial, swapped), [near, near]).reshape(width)
    return (query_grad, key_grad, value_grad, filter_grad)


def solution(mesh):
    placed = (P("ch", "ctx"), P("ch", "ctx"), P("ch", "ctx"), P("ctx"), P("ch", "ctx"))
    return jax.shard_map(
        shards,
        mesh=mesh,
        in_specs=placed,
        out_specs=(P("ch", "ctx"), P("ch", "ctx"), P("ch", "ctx"), P("ctx")),
        check_vma=False,
    )
```

```python
import math

import jax
import jax.numpy as jnp
import numpy as np
from jax import lax
from jax.experimental import pallas as pl
from jax.experimental.pallas import tpu as pltpu
from jax.sharding import PartitionSpec as P

SHIFT = 0.25
MIB = 1024 * 1024
PARTS = 2
ORDER = np.array([((1 - x) * 8 + (4 + 3 * z) % 8) * 4 + (2 + y) % 4 for z in range(8) for y in range(4) for x in range(2)])
AHEAD, BACK, TWIST = 4, 6, 7


def halves(values):
    high = values.astype(jnp.bfloat16)
    low = (values - np.asarray(high).astype(np.float64)).astype(jnp.bfloat16)
    return np.asarray(high), np.asarray(low)


def table_bank(blocks, width):
    length = blocks * width
    half = width // 2
    rows = np.arange(blocks) + SHIFT
    planes = []
    for odd in (0, 1):
        angle = 2.0 * math.pi * (np.outer(np.arange(half), 2 * np.arange(half) + odd) % width) / width
        cosine, sine = np.cos(angle), np.sin(angle)
        planes += halves(np.block([[cosine, -sine], [sine, cosine]]))
    block_angle = 2.0 * math.pi * np.outer(rows, np.arange(blocks)) / blocks
    block_table = np.concatenate([np.cos(block_angle), -np.sin(block_angle)], axis=0)
    own = [2 * ORDER + parity for parity in (0, 1)]
    for e in (0, 1):
        planes.append(np.concatenate(halves(block_table[:, own[e]]) * 2, axis=1))
    pieces = [np.concatenate(halves(block_table.T[own[e]] / length), axis=0) for e in (0, 1)]
    planes.append(np.concatenate(pieces, axis=0))
    twist_angle = 2.0 * math.pi * np.outer(rows, np.arange(width)) / length
    planes += [np.concatenate(halves(np.cos(twist_angle)), axis=0), np.concatenate(halves(np.sin(twist_angle)), axis=0)]
    return np.stack(planes)


def split(values):
    high = values.astype(jnp.bfloat16)
    return high, (values - high.astype(jnp.float32)).astype(jnp.bfloat16)


def product(left, right, transposed=False):
    contracted = (((1,), (1 if transposed else 0,)), ((), ()))
    return lax.dot_general(left, right, contracted, preferred_element_type=jnp.float32)


def inner_product(values, bank_ref, odd, transposed):
    count = values.shape[0]
    high, low = split(values)
    wide = product(jnp.concatenate([high, low], axis=0), bank_ref[2 * odd], transposed)
    return wide[:count] + wide[count:] + product(high, bank_ref[2 * odd + 1], transposed)


def fetch(pairs, arrived):
    copies = [pltpu.make_async_copy(source, here, arrived.at[i]) for i, (source, here) in enumerate(pairs)]
    for copy in copies:
        copy.start()
    return copies


def pack_body(key_far, value_far, grad_far, query_far, taps_far, out_ref, key, value, grad, query, taps, arrived):
    width = key.shape[1]
    copies = fetch(
        ((key_far, key), (value_far, value), (grad_far, grad), (query_far, query), (taps_far, taps)), arrived
    )
    copies[0].wait()
    copies[1].wait()
    out_ref[:, 0, :width] = key[...].astype(jnp.float32) * value[...].astype(jnp.float32)
    copies[2].wait()
    copies[3].wait()
    out_ref[:, 0, width : 2 * width] = grad[...].astype(jnp.float32) * query[...].astype(jnp.float32)
    copies[4].wait()
    out_ref[:, 0, 2 * width :] = jnp.broadcast_to(taps[...], key.shape)


def front_products(blocks_ref, table):
    width = table.shape[1]
    twice = jnp.concatenate([blocks_ref[:, 0, :], blocks_ref[:, 0, :]], axis=0)
    data = jnp.concatenate(split(twice), axis=0)
    return [product(table, data[:, index * width : (index + 1) * width]) for index in range(3)]


def lead_body(parity_ref, own_ref, bank_far, bank_ref, front_ref, twist_ref, arrived):
    spans = ((AHEAD, 2), (0, AHEAD), (BACK, 3))
    pairs = [(bank_far.at[pl.ds(first, count)], bank_ref.at[pl.ds(first, count)]) for first, count in spans]
    copies = fetch(pairs, arrived)
    copies[0].wait()
    for index, front in enumerate(front_products(own_ref, bank_ref[AHEAD + parity_ref[0]])):
        front_ref[index] = front
    copies[2].wait()
    rows = twist_ref.shape[1]
    for index in (0, 1):
        table = bank_ref[TWIST + index].astype(jnp.float32)
        twist_ref[index] = table[:rows] + table[rows:]
    copies[1].wait()


def middle_body(parity_ref, other_ref, front_ref, twist_ref, bank_ref, out_ref):
    parity = parity_ref[0]
    width = bank_ref.shape[2]
    half = width // 2
    rows = 2 * other_ref.shape[0]
    others = front_products(other_ref, bank_ref[AHEAD + 1 - parity])
    fronts = [front_ref[index] + others[index] for index in range(3)]
    cosine, sine = twist_ref[0], twist_ref[1]
    reals = [[] for _ in range(3)]
    imags = [[] for _ in range(3)]
    size = rows // PARTS
    stacks, spectras, mixes, outs = {}, {}, {}, {}
    pieces = [(part, bins) for bins in (0, 1) for part in range(PARTS)]

    def twisted(part):
        here = slice(part * size, (part + 1) * size)
        there = slice(rows + part * size, rows + (part + 1) * size)
        even, odd = [], []
        for index in range(3):
            real = fronts[index][here]
            imag = fronts[index][there]
            real, imag = real * cosine[here] + imag * sine[here], imag * cosine[here] - real * sine[here]
            even.append(jnp.concatenate([real[:, :half] + real[:, half:], imag[:, :half] + imag[:, half:]], axis=1))
            odd.append(jnp.concatenate([real[:, :half] - real[:, half:], imag[:, :half] - imag[:, half:]], axis=1))
        stacks[part, 0] = jnp.concatenate(even, axis=0)
        stacks[part, 1] = jnp.concatenate(odd, axis=0)

    def mix(key):
        spectra = spectras[key]
        gated_real, gated_imag = spectra[:size, :half], spectra[:size, half:]
        grad_real, grad_imag = spectra[size : 2 * size, :half], spectra[size : 2 * size, half:]
        taps_real, taps_imag = spectra[2 * size :, :half], spectra[2 * size :, half:]
        conv_real = gated_real * taps_real - gated_imag * taps_imag
        conv_imag = gated_real * taps_imag + gated_imag * taps_real
        back_real = grad_real * taps_real + grad_imag * taps_imag
        back_imag = grad_imag * taps_real - grad_real * taps_imag
        cross_real = grad_real * gated_real + grad_imag * gated_imag
        cross_imag = grad_imag * gated_real - grad_real * gated_imag
        mixes[key] = jnp.concatenate(
            [
                jnp.concatenate([conv_real, conv_imag], axis=1),
                jnp.concatenate([back_real, back_imag], axis=1),
                jnp.concatenate([cross_real, cross_imag], axis=1),
            ],
            axis=0,
        )

    def untwist(part):
        here = slice(part * size, (part + 1) * size)
        for index in range(3):
            first = outs[part, 0][index * size : (index + 1) * size]
            second = outs[part, 1][index * size : (index + 1) * size]
            total, difference = first + second, first - second
            real = jnp.concatenate([total[:, :half], difference[:, :half]], axis=1)
            imag = jnp.concatenate([total[:, half:], difference[:, half:]], axis=1)
            reals[index].append(real * cosine[here] - imag * sine[here])
            imags[index].append(real * sine[here] + imag * cosine[here])

    for part in range(PARTS):
        twisted(part)
    for key in pieces:
        spectras[key] = inner_product(stacks[key], bank_ref, key[1], False)
    for key in pieces:
        mix(key)
    for key in pieces:
        outs[key] = inner_product(mixes[key], bank_ref, key[1], True)
    for part in range(PARTS):
        untwist(part)
    table = bank_ref[BACK, pl.ds(pl.multiple_of(rows * parity, rows), rows)]
    for index in range(3):
        high, low = split(jnp.concatenate(reals[index] + imags[index], axis=0))
        wide = product(table, high)
        out_ref[:, 0, index * width : (index + 1) * width] = (
            wide[: rows // 2] + wide[rows // 2 :] + product(table[: rows // 2], low)
        )


def sum_body(scale, moved_ref, out_ref):
    width = out_ref.shape[1]
    out_ref[...] = jnp.sum(moved_ref[:, 0, 2 * width :], axis=0, keepdims=True) * scale


def finish_body(moved_ref, key_ref, value_ref, grad_ref, query_out, key_out, value_out):
    width = key_ref.shape[1]
    back = moved_ref[:, 0, width : 2 * width]
    query_out[...] = (grad_ref[...].astype(jnp.float32) * moved_ref[:, 0, :width]).astype(jnp.bfloat16)
    key_out[...] = (back * value_ref[...].astype(jnp.float32)).astype(jnp.bfloat16)
    value_out[...] = (back * key_ref[...].astype(jnp.float32)).astype(jnp.bfloat16)


def add_body(left_ref, right_ref, out_ref):
    out_ref[...] = left_ref[...] + right_ref[...]


def kernel_call(body, out_shape, limit, operands, in_specs, scratch=()):
    return pl.pallas_call(
        body,
        out_shape=out_shape,
        in_specs=in_specs,
        scratch_shapes=scratch,
        compiler_params=pltpu.CompilerParams(vmem_limit_bytes=limit * MIB),
    )(*operands)


def shards(query_proj, key_proj, value_proj, filter_taps, out_grad):
    devices = lax.axis_size("ctx")
    channels, width = query_proj.shape
    chips = devices // 2
    parity = (lax.axis_index("ctx") % 2).astype(jnp.int32).reshape(1)
    same_core = [[int(2 * chip + core) for chip in ORDER] for core in (0, 1)]
    other_core = [(device, device ^ 1) for device in range(devices)]
    scale = 1.0 / math.sqrt(channels * lax.axis_size("ch") * devices * width)
    message = jax.ShapeDtypeStruct((chips, 1, 3 * width), jnp.float32)
    narrow = jax.ShapeDtypeStruct((channels, width), jnp.bfloat16)
    bank = jnp.asarray(table_bank(devices, width))

    def exchange(array):
        return lax.all_to_all(array, "ctx", 0, 0, axis_index_groups=same_core, tiled=True)

    def channel_sum(*refs):
        sum_body(scale, *refs)

    far = pl.BlockSpec(memory_space=pltpu.HBM)
    key_far, value_far, grad_far, query_far, taps_far = [
        pltpu.with_memory_space_constraint(array, pltpu.HBM)
        for array in (key_proj, value_proj, out_grad, query_proj, filter_taps.reshape(1, width))
    ]
    near = pl.BlockSpec(memory_space=pltpu.VMEM)
    scalar = pl.BlockSpec(memory_space=pltpu.SMEM)
    local = pltpu.VMEM((channels, width), jnp.bfloat16)
    packed, key, value, grad = kernel_call(
        pack_body,
        (message, narrow, narrow, narrow),
        4,
        (key_far, value_far, grad_far, query_far, taps_far),
        [far] * 5,
        [local, pltpu.VMEM((1, width), jnp.float32), pltpu.SemaphoreType.DMA((5,))],
    )
    own = exchange(packed)
    other = lax.ppermute(own, "ctx", other_core)
    near_bank, front, twist = kernel_call(
        lead_body,
        (
            jax.ShapeDtypeStruct(bank.shape, bank.dtype),
            jax.ShapeDtypeStruct((3, 2 * devices, width), jnp.float32),
            jax.ShapeDtypeStruct((2, devices, width), jnp.float32),
        ),
        8,
        (parity, own, pltpu.with_memory_space_constraint(bank, pltpu.HBM)),
        [scalar, near, far],
        [pltpu.SemaphoreType.DMA((3,))],
    )
    restored = kernel_call(middle_body, message, 24, (parity, other, front, twist, near_bank), [scalar] + [near] * 4)
    moved = exchange(restored)
    line = jax.ShapeDtypeStruct((1, width), jnp.float32)
    partial = kernel_call(channel_sum, line, 4, (moved,), [near])
    swapped = lax.ppermute(partial, "ch", [(0, 1), (1, 0)])
    query_grad, key_grad, value_grad = kernel_call(
        finish_body, (narrow, narrow, narrow), 4, (moved, key, value, grad), [near] * 4
    )
    filter_grad = kernel_call(add_body, line, 4, (partial, swapped), [near, near]).reshape(width)
    return (query_grad, key_grad, value_grad, filter_grad)


def solution(mesh):
    placed = (P("ch", "ctx"), P("ch", "ctx"), P("ch", "ctx"), P("ctx"), P("ch", "ctx"))
    return jax.shard_map(
        shards,
        mesh=mesh,
        in_specs=placed,
        out_specs=(P("ch", "ctx"), P("ch", "ctx"), P("ch", "ctx"), P("ctx")),
        check_vma=False,
    )
```
